256 devices in a mesh: seq: 16 (over z, core), own: 16 (over x, y).
Axes of the slice: x: 4, y: 4, z: 8, core: 2. Of those that a mesh axis runs over, the one named last changes fastest.
Arguments:
- query_rows: bfloat16 [16, 2048, 2048], P('own', 'seq'), may hold values from -9 to 9
- key_rows: bfloat16 [16, 2048, 2048], P('own', 'seq'), may hold values from -9 to 9
- value_rows: bfloat16 [16, 2048, 2048], P('own', 'seq'), may hold values from -16 to 16
- out_grad: bfloat16 [16, 2048, 2048], P('own', 'seq'), may hold values from -6 to 6
- norm_gains: float32 [2048], P('own'), may hold values from 0.1 to 1.9
- window: int32 [16], P('seq'), may hold values from 0 to 2, as said below
- global_blocks: int32 [16, 2], P('own'), may hold values from 0 to 31, as said below
- random_blocks: int32 [16, 32, 3], P('seq'), may hold values from 0 to 31
Outputs:
- grad_q: bfloat16 [16, 2048, 2048], P('own', 'seq')
- grad_k: bfloat16 [16, 2048, 2048], P('own', 'seq')
- grad_v: bfloat16 [16, 2048, 2048], P('own', 'seq')
- gain_grad: float32 [2048], P('seq')
The draws below stay inside these ranges and needn't reach their ends.
Inputs may be any that keep to these rules, and one draw needn't show every extreme that they name: `window`: some head reaches 2 blocks on either side in every draw. `global_blocks`: the 2 global blocks of a filing are distinct.
All inputs are finite; a program needn't handle non-finite values.
Results may differ from the reference program's by a relative error of at most 0.012.
Values may be sent and summed in bfloat16 or wider, within the bound.
No kernel may reach another device: no remote copies, remote signals or barrier semaphores. Data moves between devices by JAX's collectives and lax.ppermute only.
A program may use at most 128 MiB of HBM per device.

```python
import math
import jax
import jax.numpy as jnp
from jax import lax

HEADS = 16
HDIM = 128
BLK = 64
WMAX = 2
GLOB = 2
RAND = 3
SEQ = 2048
NB = 32
FILINGS = 16


def draw_query_rows(key, part):
    base_noise = jax.random.truncated_normal(jax.random.fold_in(key, 11), -6.0, 6.0, (FILINGS, SEQ, HEADS * HDIM), jnp.float32)
    return base_noise.astype(jnp.bfloat16)


def draw_key_rows(key, part):
    base_noise = jax.random.truncated_normal(jax.random.fold_in(key, 12), -6.0, 6.0, (FILINGS, SEQ, HEADS * HDIM), jnp.float32)
    return base_noise.astype(jnp.bfloat16)


def draw_value_rows(key, part):
    head_of_column = (jnp.arange(HEADS * HDIM) // HDIM).astype(jnp.float32)
    head_scale = 0.4 * 10.0 ** (head_of_column / (HEADS - 1))
    base_noise = jax.random.truncated_normal(jax.random.fold_in(key, 13), -4.0, 4.0, (FILINGS, SEQ, HEADS * HDIM), jnp.float32)
    return (base_noise * head_scale[None, None, :]).astype(jnp.bfloat16)


def draw_window(key, part):
    widths = jax.random.randint(jax.random.fold_in(key, 21), (HEADS,), 0, WMAX + 1)
    chosen = jax.random.randint(jax.random.fold_in(key, 22), (), 0, HEADS)
    widths = jnp.where(jnp.arange(HEADS) == chosen, WMAX, widths)
    return widths.astype(jnp.int32)


def draw_global_blocks(key, part):
    filing_keys = jax.random.split(jax.random.fold_in(key, 31), FILINGS)

    def pick(subkey):
        return jax.random.permutation(subkey, SEQ // BLK)[:GLOB]
    return jax.vmap(pick)(filing_keys).astype(jnp.int32)


def place_ends(values, key, least, top_value):
    place = [jax.random.randint(jax.random.fold_in(key, axis), (), 0, length) for axis, length in enumerate(values.shape)]
    longest = values.shape.index(max(values.shape))
    next_to = place[:longest] + [(place[longest] + 1) % values.shape[longest]] + place[longest + 1:]
    return values.at[tuple(place)].set(least).at[tuple(next_to)].set(top_value)


def with_spikes(array, own_key, source, target, blocks, factor):
    def block_of(axis_at):
        return (jnp.arange(array.shape[axis_at]) // (array.shape[axis_at] // blocks)).reshape((-1,) + (1,) * (array.ndim - 1 - axis_at))

    near = jax.random.permutation(own_key, blocks)[block_of(target)]
    second = (block_of(target) + blocks // 2) % blocks
    return jnp.where((block_of(source) == near) | (block_of(source) == second), factor * array, array)


def level_of(stream_key, extent, pieces, least, largest):
    def one(axis_at, shards_of):
        draws = jax.random.uniform(jax.random.fold_in(jax.random.fold_in(stream_key, 6), axis_at), (shards_of,), jnp.float32, least / len(pieces), largest / len(pieces))
        return jnp.repeat(jnp.exp(draws), extent[axis_at] // shards_of).reshape((-1,) + (1,) * (len(extent) - axis_at - 1))

    gain = one(*pieces[0])
    for cut in pieces[1:]:
        gain = gain * one(*cut)
    return gain


def heavy_noise(stream_key, dims, width, bound, pieces, heavy, kind=jnp.bfloat16):
    entries = width * jax.random.normal(stream_key, dims, jnp.float32)
    if pieces:
        entries = entries * level_of(stream_key, dims, pieces, -0.22, 0.18)
    return jnp.clip(with_spikes(entries, jax.random.fold_in(stream_key, 3), *heavy), -bound, bound).astype(kind)


def setup_inputs(seed: int = 0) -> dict:
    keys = jax.random.split(jax.random.key(seed), 9)
    query_rows = draw_query_rows(jax.random.fold_in(keys[8], 71), 0)
    key_rows = draw_key_rows(jax.random.fold_in(keys[8], 71), 0)
    value_rows = draw_value_rows(jax.random.fold_in(keys[8], 71), 0)
    out_grad = heavy_noise(keys[3], (FILINGS, SEQ, HEADS * HDIM), 1.0, 6.0, ((0, 16), (1, 16)), (1, 2, 16, 2.0))
    norm_gains = jnp.clip(1.0 + 0.18 * jax.random.normal(keys[4], (HEADS * HDIM,), jnp.float32), 0.1, 1.9)
    window = draw_window(jax.random.fold_in(keys[8], 71), 0)
    global_blocks = draw_global_blocks(jax.random.fold_in(keys[8], 71), 0)
    random_blocks = place_ends(jax.random.randint(keys[7], (HEADS, NB, RAND), 0, NB), jax.random.fold_in(keys[7], 1), 0, NB - 1).astype(jnp.int32)
    return dict(query_rows=query_rows, key_rows=key_rows, value_rows=value_rows, out_grad=out_grad, norm_gains=norm_gains, window=window, global_blocks=global_blocks, random_blocks=random_blocks)


NEG_FILL = -1e+30
EPSILON = 1e-05

def rounded(values):
    return lax.optimization_barrier(values.astype(jnp.bfloat16))

def slot_table(head_width, filing_globals, head_random, block_count):
    block_index = jnp.arange(block_count, dtype=jnp.int32)[:, None]
    offsets = jnp.arange(-WMAX, WMAX + 1, dtype=jnp.int32)[None, :]
    near_ids = block_index + offsets
    near_live = (jnp.abs(offsets) <= head_width) & (near_ids >= 0) & (near_ids < block_count)
    near_ids = jnp.clip(near_ids, 0, block_count - 1).astype(jnp.int32)
    global_ids = jnp.broadcast_to(filing_globals[None, :].astype(jnp.int32), (block_count, GLOB))
    slot_ids = jnp.concatenate([near_ids, global_ids, head_random.astype(jnp.int32)], axis=1)
    slot_live = jnp.concatenate([near_live, jnp.ones((block_count, GLOB + RAND), dtype=jnp.bool_)], axis=1)
    slot_count = slot_ids.shape[1]
    earlier_slot = jnp.arange(slot_count)[:, None] > jnp.arange(slot_count)[None, :]
    repeated = jnp.any((slot_ids[:, :, None] == slot_ids[:, None, :]) & earlier_slot[None, :, :] & slot_live[:, None, :], axis=2)
    return (slot_ids, slot_live & jnp.logical_not(repeated))

def gather_slots(source_rows, slot_ids):
    block_count = slot_ids.shape[0]
    blocked = source_rows.reshape(block_count, BLK, source_rows.shape[-1])
    return blocked[slot_ids].reshape(block_count, slot_ids.shape[1] * BLK, source_rows.shape[-1])

def masked_softmax(scores, live_mask):
    masked = jnp.where(live_mask, scores, NEG_FILL)
    row_max = lax.optimization_barrier(jnp.max(masked, axis=-1, keepdims=True))
    weights = jnp.where(live_mask, jnp.exp(masked - row_max), 0.0)
    return weights / lax.optimization_barrier(jnp.sum(weights, axis=-1, keepdims=True))

def head_probs(query_h, key_h, head_width, filing_globals, head_random):
    row_count = query_h.shape[0]
    block_count = row_count // BLK
    slot_ids, slot_live = slot_table(head_width, filing_globals, head_random, block_count)
    score_scale = 1.0 / math.sqrt(HDIM)
    query_blocks = query_h.astype(jnp.float32).reshape(block_count, BLK, HDIM)
    slot_keys = gather_slots(key_h, slot_ids).astype(jnp.float32)
    sparse_scores = jnp.einsum('nqd,nkd->nqk', query_blocks, slot_keys) * score_scale
    key_live = jnp.repeat(slot_live, BLK, axis=1)[:, None, :]
    sparse_probs = masked_softmax(sparse_scores, key_live)
    is_global = jnp.any(jnp.arange(block_count, dtype=jnp.int32)[:, None] == filing_globals[None, :], axis=1)
    sparse_probs = jnp.where(is_global[:, None, None], 0.0, sparse_probs)
    global_scores = jnp.einsum('gqd,kd->gqk', query_blocks[filing_globals], key_h.astype(jnp.float32)) * score_scale
    global_probs = masked_softmax(global_scores, jnp.ones((row_count,), dtype=jnp.bool_))
    return (slot_ids, sparse_probs, global_probs)

def head_forward(query_h, key_h, value_h, head_width, filing_globals, head_random):
    row_count = query_h.shape[0]
    slot_ids, sparse_probs, global_probs = head_probs(query_h, key_h, head_width, filing_globals, head_random)
    slot_values = gather_slots(value_h, slot_ids).astype(jnp.float32)
    sparse_out = jnp.einsum('nqk,nkd->nqd', rounded(sparse_probs).astype(jnp.float32), slot_values)
    global_out = jnp.einsum('gqk,kd->gqd', rounded(global_probs).astype(jnp.float32), value_h.astype(jnp.float32))
    attention = sparse_out.at[filing_globals].set(global_out)
    return rounded(attention.reshape(row_count, HDIM))

def head_backward(query_h, key_h, value_h, grad_h, attn_h, head_width, filing_globals, head_random):
    row_count = query_h.shape[0]
    block_count = row_count // BLK
    score_scale = 1.0 / math.sqrt(HDIM)
    slot_ids, sparse_probs, global_probs = head_probs(query_h, key_h, head_width, filing_globals, head_random)
    slot_count = slot_ids.shape[1]
    probs_low = rounded(sparse_probs).astype(jnp.float32)
    global_low = rounded(global_probs).astype(jnp.float32)
    query_blocks = query_h.astype(jnp.float32).reshape(block_count, BLK, HDIM)
    grad_blocks = grad_h.astype(jnp.float32).reshape(block_count, BLK, HDIM)
    slot_keys = gather_slots(key_h, slot_ids).astype(jnp.float32)
    slot_values = gather_slots(value_h, slot_ids).astype(jnp.float32)
    value_slots = jnp.einsum('nqk,nqd->nkd', probs_low, grad_blocks).reshape(block_count, slot_count, BLK, HDIM)
    grad_value = jnp.zeros((block_count, BLK, HDIM), jnp.float32).at[slot_ids].add(value_slots).reshape(row_count, HDIM)
    global_grad_rows = grad_blocks[filing_globals]
    grad_value = grad_value + jnp.einsum('gqk,gqd->kd', global_low, global_grad_rows)
    row_dot = lax.optimization_barrier(jnp.sum(grad_h.astype(jnp.float32) * attn_h.astype(jnp.float32), axis=-1)).reshape(block_count, BLK)
    prob_grad = jnp.einsum('nqd,nkd->nqk', grad_blocks, slot_values)
    score_grad = rounded(sparse_probs * (prob_grad - row_dot[:, :, None]) * score_scale).astype(jnp.float32)
    grad_query = jnp.einsum('nqk,nkd->nqd', score_grad, slot_keys)
    key_slots = jnp.einsum('nqk,nqd->nkd', score_grad, query_blocks).reshape(block_count, slot_count, BLK, HDIM)
    grad_key = jnp.zeros((block_count, BLK, HDIM), jnp.float32).at[slot_ids].add(key_slots).reshape(row_count, HDIM)
    global_prob_grad = jnp.einsum('gqd,kd->gqk', global_grad_rows, value_h.astype(jnp.float32))
    global_score_grad = rounded(global_probs * (global_prob_grad - row_dot[filing_globals][:, :, None]) * score_scale).astype(jnp.float32)
    global_query_grad = jnp.einsum('gqk,kd->gqd', global_score_grad, key_h.astype(jnp.float32))
    grad_query = grad_query.at[filing_globals].set(global_query_grad).reshape(row_count, HDIM)
    grad_key = grad_key + jnp.einsum('gqk,gqd->kd', global_score_grad, query_blocks[filing_globals])
    return (grad_query.astype(jnp.bfloat16), grad_key.astype(jnp.bfloat16), grad_value.astype(jnp.bfloat16))

def split_heads(flat_rows):
    return flat_rows.reshape(flat_rows.shape[0], HEADS, HDIM).transpose(1, 0, 2)

def join_heads(stacked):
    return stacked.transpose(1, 0, 2).reshape(stacked.shape[1], HEADS * HDIM)

def reference(query_rows, key_rows, value_rows, out_grad, norm_gains, window, global_blocks, random_blocks):

    def filing_pass(filing_data):
        query_f, key_f, value_f, grad_f, filing_globals = filing_data
        filing_globals = filing_globals.astype(jnp.int32)

        def forward_head(head_data):
            query_h, key_h, value_h, head_width, head_random = head_data
            return head_forward(query_h, key_h, value_h, head_width, filing_globals, head_random)
        attention = join_heads(lax.map(forward_head, (split_heads(query_f), split_heads(key_f), split_heads(value_f), window, random_blocks)))
        attn_wide = attention.astype(jnp.float32)
        grad_wide = grad_f.astype(jnp.float32)
        inv_rms = lax.rsqrt(lax.optimization_barrier(jnp.mean(attn_wide * attn_wide, axis=-1, keepdims=True)) + EPSILON)
        scaled_grad = norm_gains[None, :] * grad_wide
        inner_mean = lax.optimization_barrier(jnp.mean(scaled_grad * attn_wide, axis=-1, keepdims=True))
        attn_grad = rounded(inv_rms * (scaled_grad - attn_wide * (inv_rms * inv_rms) * inner_mean))
        gain_terms = lax.optimization_barrier(jnp.sum(grad_wide * attn_wide * inv_rms, axis=0))

        def backward_head(head_data):
            query_h, key_h, value_h, grad_h, attn_h, head_width, head_random = head_data
            return head_backward(query_h, key_h, value_h, grad_h, attn_h, head_width, filing_globals, head_random)
        grad_query, grad_key, grad_value = lax.map(backward_head, (split_heads(query_f), split_heads(key_f), split_heads(value_f), split_heads(attn_grad), split_heads(attention), window, random_blocks))
        return (join_heads(grad_query), join_heads(grad_key), join_heads(grad_value), gain_terms)
    grad_query, grad_key, grad_value, gain_terms = lax.map(filing_pass, (query_rows, key_rows, value_rows, out_grad, global_blocks))
    gain_grad = lax.optimization_barrier(jnp.sum(gain_terms, axis=0)) * (FILINGS * SEQ) ** (-0.5)
    return (grad_query, grad_key, grad_value, gain_grad)
```

```python
import functools
import math

import jax
import jax.numpy as jnp
from jax import lax
from jax.experimental import pallas as pl
from jax.experimental.pallas import tpu as pltpu
from jax.sharding import PartitionSpec as P

HDIM = 128
BLK = 64
NEG_FILL = -1e30
EPSILON = 1e-05
QTILE = 256
KTILE = 256
VMEM_LIMIT = 48 * 1024 * 1024


def pack_kernel(q_ref, k_ref, v_ref, g_ref, out_ref):
    heads = out_ref.shape[0]
    rows = q_ref.shape[1]
    for slot, ref in enumerate((q_ref, k_ref, v_ref, g_ref)):
        for h in range(heads):
            out_ref[h, slot * rows:(slot + 1) * rows, :] = ref[0, :, h * HDIM:(h + 1) * HDIM]


def pack(query_rows, key_rows, value_rows, out_grad):
    _, rows, cols = query_rows.shape
    heads = cols // HDIM
    steps = 4
    spec = pl.BlockSpec((1, rows, cols // steps), lambda i: (0, 0, i))
    return pl.pallas_call(
        pack_kernel,
        grid=(steps,),
        out_shape=jax.ShapeDtypeStruct((heads, 4 * rows, HDIM), query_rows.dtype),
        in_specs=[spec] * 4,
        out_specs=pl.BlockSpec((heads // steps, 4 * rows, HDIM), lambda i: (i, 0, 0)),
        name="pack",
    )(query_rows, key_rows, value_rows, out_grad)


def unpack_kernel(in_ref, q_ref, k_ref, v_ref):
    heads = in_ref.shape[0]
    rows = q_ref.shape[1]
    for slot, ref in enumerate((q_ref, k_ref, v_ref)):
        for h in range(heads):
            ref[0, :, h * HDIM:(h + 1) * HDIM] = in_ref[h, slot * rows:(slot + 1) * rows, :]


def unpack(exchanged):
    heads, rows3, _ = exchanged.shape
    rows = rows3 // 3
    steps = 4
    spec = pl.BlockSpec((1, rows, heads * HDIM // steps), lambda i: (0, 0, i))
    shape = jax.ShapeDtypeStruct((1, rows, heads * HDIM), exchanged.dtype)
    return pl.pallas_call(
        unpack_kernel,
        grid=(steps,),
        out_shape=[shape] * 3,
        in_specs=[pl.BlockSpec((heads // steps, rows3, HDIM), lambda i: (i, 0, 0))],
        out_specs=[spec] * 3,
        name="unpack",
    )(exchanged)


def forward_kernel(
    q_ref, k_ref, v_ref, g_ref, bias_ref, gain_ref,
    e_ref, attn_ref, inv_ref, stat_ref,
    vt_ref, s_ref,
):
    seq = s_ref.shape[0]
    devs = stat_ref.shape[0]

    @pl.when(pl.program_id(0) == 0)
    def _():
        for i in range(v_ref.shape[0]):
            vt_ref[:, i * 128:(i + 1) * 128] = v_ref[i].astype(jnp.float32).T.astype(jnp.bfloat16)

    q = q_ref[...].reshape(QTILE, HDIM)
    top = jnp.full((8, QTILE), NEG_FILL, jnp.float32)
    for c in range(seq // KTILE):
        keys = k_ref[c * 2:(c + 1) * 2].reshape(KTILE, HDIM)
        s = lax.dot_general(keys, q, (((1,), (1,)), ((), ())), preferred_element_type=jnp.float32)
        for b in range(KTILE // BLK):
            row = c * (KTILE // BLK) + b
            sb = s[b * BLK:(b + 1) * BLK] + bias_ref[row:row + 1, :]
            s_ref[row * BLK:(row + 1) * BLK, :] = sb
            top = jnp.maximum(top, jnp.max(sb.reshape(BLK // 8, 8, QTILE), axis=0))
    top = jnp.max(top, axis=0, keepdims=True)
    factor = math.log2(math.e) / math.sqrt(HDIM)
    total = jnp.zeros((8, QTILE), jnp.float32)
    for c in range(seq // KTILE):
        e = jnp.exp2((s_ref[c * KTILE:(c + 1) * KTILE, :] - top) * factor)
        total = total + jnp.sum(e.reshape(KTILE // 8, 8, QTILE), axis=0)
        e_ref[c * KTILE:(c + 1) * KTILE, :] = e.astype(jnp.bfloat16)
    inv = 1.0 / jnp.sum(total, axis=0, keepdims=True)
    attn = jnp.dot(vt_ref[...], e_ref[...], preferred_element_type=jnp.float32) * inv
    attn = attn.astype(jnp.bfloat16)
    attn_ref[...] = attn
    inv_ref[...] = inv
    attn = attn.astype(jnp.float32)
    grad = g_ref[...].reshape(QTILE, HDIM).astype(jnp.float32).T
    stats = jnp.concatenate(
        [
            jnp.sum(attn * attn, axis=0, keepdims=True),
            jnp.sum(gain_ref[...] * grad * attn, axis=0, keepdims=True),
        ],
        axis=0,
    )
    for d in range(devs):
        stat_ref[d] = stats


def forward(exchanged, bias, gain_col):
    devs, rows4, _ = exchanged.shape
    rows = rows4 // 4
    seq = devs * rows
    per = QTILE // rows
    whole = lambda slot: pl.BlockSpec((devs, rows, HDIM), lambda j: (0, slot, 0))
    part = lambda slot: pl.BlockSpec((per, rows, HDIM), lambda j: (j, slot, 0))
    return pl.pallas_call(
        forward_kernel,
        grid=(seq // QTILE,),
        out_shape=[
            jax.ShapeDtypeStruct((seq, seq), jnp.bfloat16),
            jax.ShapeDtypeStruct((HDIM, seq), jnp.bfloat16),
            jax.ShapeDtypeStruct((1, seq), jnp.float32),
            jax.ShapeDtypeStruct((devs, 2, seq), jnp.float32),
        ],
        in_specs=[
            part(0), whole(1), whole(2), part(3),
            pl.BlockSpec((seq // BLK, QTILE), lambda j: (0, j)),
            pl.BlockSpec((HDIM, 1), lambda j: (0, 0)),
        ],
        out_specs=[
            pl.BlockSpec((seq, QTILE), lambda j: (0, j)),
            pl.BlockSpec((HDIM, QTILE), lambda j: (0, j)),
            pl.BlockSpec((1, QTILE), lambda j: (0, j)),
            pl.BlockSpec((devs, 2, QTILE), lambda j: (0, 0, j)),
        ],
        scratch_shapes=[
            pltpu.VMEM((HDIM, seq), jnp.bfloat16),
            pltpu.VMEM((seq, QTILE), jnp.float32),
        ],
        compiler_params=pltpu.CompilerParams(vmem_limit_bytes=VMEM_LIMIT),
        name="forward",
    )(exchanged, exchanged, exchanged, exchanged, bias, gain_col)


def backward_kernel(
    q_ref, k_ref, v_ref, g_ref, e_ref, attn_ref, inv_ref, stat_ref, gain_ref,
    out_ref, gain_out_ref,
    kt_ref, ds_ref, dk_ref, dv_ref,
):
    j = pl.program_id(0)
    devs, rows, _ = k_ref.shape
    seq = devs * rows
    cols = seq
    scale = 1.0 / math.sqrt(HDIM)

    @pl.when(j == 0)
    def _():
        for i in range(devs):
            kt_ref[:, i * 128:(i + 1) * 128] = k_ref[i].astype(jnp.float32).T.astype(jnp.bfloat16)
        dk_ref[...] = jnp.zeros_like(dk_ref)
        dv_ref[...] = jnp.zeros_like(dv_ref)
        gain_out_ref[...] = jnp.zeros_like(gain_out_ref)

    width = devs * HDIM
    stats = jnp.sum(stat_ref[...], axis=0) * (1.0 / width)
    inv_rms = lax.rsqrt(stats[0:1] + EPSILON)
    inner = stats[1:2]
    attn = attn_ref[...].astype(jnp.float32)
    grad = g_ref[...].reshape(QTILE, HDIM).astype(jnp.float32).T
    q = q_ref[...].reshape(QTILE, HDIM)
    attn_grad = inv_rms * (gain_ref[...] * grad - attn * (inv_rms * inv_rms) * inner)
    gain_out_ref[...] += jnp.sum(grad * attn * inv_rms, axis=1, keepdims=True)
    low = (attn_grad * inv_ref[...]).astype(jnp.bfloat16)
    row_dot = jnp.sum(low.astype(jnp.float32) * attn, axis=0, keepdims=True)
    for c in range(seq // KTILE):
        span = slice(c * KTILE, (c + 1) * KTILE)
        e = e_ref[span, :]
        values = v_ref[c * 2:(c + 1) * 2].reshape(KTILE, HDIM)
        dp = jnp.dot(values, low, preferred_element_type=jnp.float32)
        ds = (e.astype(jnp.float32) * (dp - row_dot)).astype(jnp.bfloat16)
        ds_ref[span, :] = ds
        dk_ref[span, :] += jnp.dot(ds, q, preferred_element_type=jnp.float32)
        dv_ref[span, :] += lax.dot_general(
            e, low, (((1,), (1,)), ((), ())), preferred_element_type=jnp.float32
        )
    dq = jnp.dot(kt_ref[...], ds_ref[...], preferred_element_type=jnp.float32) * scale
    dq = dq.T.astype(jnp.bfloat16)
    per = QTILE // rows
    for i in range(per):
        out_ref[j * per + i, 0:rows, :] = dq[i * rows:(i + 1) * rows]

    @pl.when(j == pl.num_programs(0) - 1)
    def _():
        for i in range(devs):
            span = slice(i * rows, (i + 1) * rows)
            out_ref[i, rows:2 * rows, :] = (dk_ref[span, :] * scale).astype(jnp.bfloat16)
            out_ref[i, 2 * rows:3 * rows, :] = dv_ref[span, :].astype(jnp.bfloat16)


def backward(exchanged, weights, attn_t, inv_sum, stats, gain_col):
    devs, rows4, _ = exchanged.shape
    rows = rows4 // 4
    seq = devs * rows
    per = QTILE // rows
    whole = lambda slot: pl.BlockSpec((devs, rows, HDIM), lambda j: (0, slot, 0))
    part = lambda slot: pl.BlockSpec((per, rows, HDIM), lambda j: (j, slot, 0))
    return pl.pallas_call(
        backward_kernel,
        grid=(seq // QTILE,),
        out_shape=[
            jax.ShapeDtypeStruct((devs, 3 * rows, HDIM), jnp.bfloat16),
            jax.ShapeDtypeStruct((HDIM, 1), jnp.float32),
        ],
        in_specs=[
            part(0), whole(1), whole(2), part(3),
            pl.BlockSpec((seq, QTILE), lambda j: (0, j)),
            pl.BlockSpec((HDIM, QTILE), lambda j: (0, j)),
            pl.BlockSpec((1, QTILE), lambda j: (0, j)),
            pl.BlockSpec((devs, 2, QTILE), lambda j: (0, 0, j)),
            pl.BlockSpec((HDIM, 1), lambda j: (0, 0)),
        ],
        out_specs=[
            pl.BlockSpec((devs, 3 * rows, HDIM), lambda j: (0, 0, 0)),
            pl.BlockSpec((HDIM, 1), lambda j: (0, 0)),
        ],
        scratch_shapes=[
            pltpu.VMEM((HDIM, seq), jnp.bfloat16),
            pltpu.VMEM((seq, QTILE), jnp.bfloat16),
            pltpu.VMEM((seq, HDIM), jnp.float32),
            pltpu.VMEM((seq, HDIM), jnp.float32),
        ],
        compiler_params=pltpu.CompilerParams(vmem_limit_bytes=VMEM_LIMIT),
        name="backward",
    )(exchanged, exchanged, exchanged, exchanged, weights, attn_t, inv_sum, stats, gain_col)


def mask_bias(head_width, filing_globals, head_random, seq):
    count = seq // BLK
    keys = jnp.arange(count, dtype=jnp.int32)[:, None]
    queries = jnp.arange(count, dtype=jnp.int32)[None, :]
    allowed = jnp.abs(keys - queries) <= head_width
    for g in range(filing_globals.shape[0]):
        allowed = allowed | (keys == filing_globals[g]) | (queries == filing_globals[g])
    for r in range(head_random.shape[1]):
        allowed = allowed | (keys == head_random[:, r][None, :])
    return jnp.repeat(jnp.where(allowed, 0.0, NEG_FILL).astype(jnp.float32), BLK, axis=1)


def body(
    query_rows, key_rows, value_rows, out_grad, norm_gains, window, global_blocks, random_blocks
):
    seq_count = lax.axis_size("seq")
    own_count = lax.axis_size("own")
    rows = query_rows.shape[1]
    seq = rows * seq_count
    gain_scale = (own_count * seq) ** (-0.5)
    exchange = functools.partial(
        lax.all_to_all, axis_name="seq", split_axis=0, concat_axis=0, tiled=True
    )
    packed = pack(query_rows, key_rows, value_rows, out_grad)
    exchanged = exchange(packed)
    swap = [(o * own_count + s, s * own_count + o) for s in range(seq_count) for o in range(own_count)]
    gain_col = lax.ppermute(norm_gains, ("seq", "own"), swap).reshape(-1, 1)
    bias = mask_bias(window[0], global_blocks[0], random_blocks[0], seq)
    weights, attn_t, inv_sum, stats = forward(exchanged, bias, gain_col)
    stats = exchange(stats)
    grads, gain_part = backward(exchanged, weights, attn_t, inv_sum, stats, gain_col)
    gain_terms = lax.all_gather(gain_part.reshape(-1), "own")
    gain_grad = jnp.sum(gain_terms, axis=0) * gain_scale
    out_query, out_key, out_value = unpack(exchange(grads))
    return (out_query, out_key, out_value, gain_grad)


def solution(mesh):
    rows = P("own", "seq", None)
    placed = (rows, rows, rows, rows, P("own"), P("seq"), P("own", None), P("seq", None, None))
    return jax.shard_map(
        body,
        mesh=mesh,
        in_specs=placed,
        out_specs=(rows, rows, rows, P("seq")),
        check_vma=False,
    )
```

```python
import functools
import math

import jax
import jax.numpy as jnp
from jax import lax
from jax.experimental import pallas as pl
from jax.experimental.pallas import tpu as pltpu
from jax.sharding import PartitionSpec as P

HDIM = 128
BLK = 64
WMAX = 2
PAIR = 2
GROUP = 8
NEG_FILL = -1e30
EPSILON = 1e-05
SCALE = 1.0 / math.sqrt(HDIM)
EXP_FACTOR = math.log2(math.e) * SCALE
VMEM_LIMIT = 40 * 1024 * 1024

NT = (((1,), (1,)), ((), ()))
TN = (((0,), (0,)), ((), ()))


def dot(a, b, dims=None):
    if dims is None:
        return jnp.dot(a, b, preferred_element_type=jnp.float32)
    return lax.dot_general(a, b, dims, preferred_element_type=jnp.float32)


def pack_kernel(q_ref, k_ref, v_ref, g_ref, out_ref, sems):
    heads = out_ref.shape[0]
    rows = q_ref.shape[1]
    copies = [
        pltpu.make_async_copy(
            ref.at[0, :, h * HDIM:(h + 1) * HDIM],
            out_ref.at[h, slot * rows:(slot + 1) * rows, :],
            sems.at[slot, h],
        )
        for slot, ref in enumerate((q_ref, k_ref, v_ref, g_ref))
        for h in range(heads)
    ]
    for copy in copies:
        copy.start()
    for copy in copies:
        copy.wait()


def pack(query_rows, key_rows, value_rows, out_grad):
    _, rows, cols = query_rows.shape
    heads = cols // HDIM
    return pl.pallas_call(
        pack_kernel,
        out_shape=jax.ShapeDtypeStruct((heads, 4 * rows, HDIM), query_rows.dtype),
        in_specs=[pl.BlockSpec(memory_space=pltpu.HBM)] * 4,
        out_specs=pl.BlockSpec(memory_space=pltpu.HBM),
        scratch_shapes=[pltpu.SemaphoreType.DMA((4, heads))],
        name="pack",
    )(query_rows, key_rows, value_rows, out_grad)


def unpack_kernel(in_ref, q_ref, k_ref, v_ref, sems):
    heads = in_ref.shape[0]
    rows = q_ref.shape[1]
    copies = [
        pltpu.make_async_copy(
            in_ref.at[h, slot * rows:(slot + 1) * rows, :],
            ref.at[0, :, h * HDIM:(h + 1) * HDIM],
            sems.at[slot, h],
        )
        for slot, ref in enumerate((q_ref, k_ref, v_ref))
        for h in range(heads)
    ]
    for copy in copies:
        copy.start()
    for copy in copies:
        copy.wait()


def unpack(exchanged):
    heads, rows3, _ = exchanged.shape
    rows = rows3 // 3
    shape = jax.ShapeDtypeStruct((1, rows, heads * HDIM), exchanged.dtype)
    return pl.pallas_call(
        unpack_kernel,
        out_shape=[shape] * 3,
        in_specs=[pl.BlockSpec(memory_space=pltpu.VMEM)],
        out_specs=[pl.BlockSpec(memory_space=pltpu.HBM)] * 3,
        scratch_shapes=[pltpu.SemaphoreType.DMA((3, heads))],
        name="unpack",
    )(exchanged)


def block_rows(ref, block, slot, rows):
    per = rows // BLK
    offset = pl.multiple_of(slot * rows + (block % per) * BLK, BLK)
    return ref[block // per, pl.ds(offset, BLK), :]


def all_rows(ref, slot, rows):
    return ref[:, slot * rows:(slot + 1) * rows, :].reshape(ref.shape[0] * rows, HDIM)


def forward_kernel(
    slots_ref, globs_ref, local_ref, in_ref, bias_ref, gain_ref,
    probs_ref, dense_ref, attn_ref, stat_ref,
    s_ref, sd_ref,
):
    devs, rows4, _ = in_ref.shape
    rows = rows4 // 4
    count = slots_ref.shape[1]
    globs = globs_ref.shape[0]
    width = count * BLK
    seq = devs * rows

    def gather(pair, slot):
        return jnp.concatenate(
            [block_rows(in_ref, slots_ref[pair, t], slot, rows) for t in range(count)], axis=0
        )

    def group(step, carry):
        pairs = [step * GROUP + u for u in range(GROUP)]
        tops = []
        for u, pair in enumerate(pairs):
            q = in_ref[pair, 0:rows, :]
            s = dot(q, gather(pair, 1), NT)
            s = jnp.concatenate(
                [s[b * BLK:(b + 1) * BLK] + bias_ref[pair, b:b + 1, :] for b in range(PAIR)], axis=0
            )
            s_ref[u] = s
            tops.append(jnp.max(s, axis=1, keepdims=True))
        sums = []
        for u, pair in enumerate(pairs):
            e = jnp.exp2((s_ref[u] - tops[u]) * EXP_FACTOR)
            s_ref[u] = e
            sums.append(jnp.sum(e, axis=1, keepdims=True))
        for u, pair in enumerate(pairs):
            row = lax.broadcasted_iota(jnp.int32, (rows, 1), 0)
            local = jnp.where(row < BLK, local_ref[pair, 0], local_ref[pair, 1])
            probs = (s_ref[u] * (local / sums[u])).astype(jnp.bfloat16)
            probs_ref[pair] = probs
            attn_ref[pair] = dot(probs, gather(pair, 2)).astype(jnp.bfloat16)
        return carry

    lax.fori_loop(0, devs // GROUP, group, 0)

    q = jnp.concatenate([block_rows(in_ref, globs_ref[t], 0, rows) for t in range(globs)], axis=0)
    step = 512
    tops = []
    for c in range(seq // step):
        keys = in_ref[c * 4:(c + 1) * 4, rows:2 * rows, :].reshape(step, HDIM)
        s = dot(q, keys, NT)
        sd_ref[:, c * step:(c + 1) * step] = s
        tops.append(jnp.max(s, axis=1, keepdims=True))
    top = functools.reduce(jnp.maximum, tops)
    total = jnp.zeros((globs * BLK, 1), jnp.float32)
    for c in range(seq // step):
        e = jnp.exp2((sd_ref[:, c * step:(c + 1) * step] - top) * EXP_FACTOR)
        sd_ref[:, c * step:(c + 1) * step] = e
        total = total + jnp.sum(e, axis=1, keepdims=True)
    inv = 1.0 / total
    for c in range(seq // step):
        dense_ref[:, c * step:(c + 1) * step] = (
            sd_ref[:, c * step:(c + 1) * step] * inv
        ).astype(jnp.bfloat16)
    out = dot(dense_ref[...], all_rows(in_ref, 2, rows)).astype(jnp.bfloat16)
    per = rows // BLK
    for t in range(globs):
        block = globs_ref[t]
        attn_ref[block // per, pl.ds(pl.multiple_of((block % per) * BLK, BLK), BLK), :] = (
            out[t * BLK:(t + 1) * BLK]
        )

    for i in range(devs):
        attn = attn_ref[i].astype(jnp.float32)
        grad = in_ref[i, 3 * rows:4 * rows, :].astype(jnp.float32) * gain_ref[...]
        square = jnp.sum((attn * attn).T, axis=0, keepdims=True)
        inner = jnp.sum((grad * attn).T, axis=0, keepdims=True)
        stats = jnp.concatenate([square, inner], axis=0)
        for d in range(devs):
            stat_ref[d, :, i * rows:(i + 1) * rows] = stats


def forward(slots, globs, local, exchanged, bias, gain_row):
    devs, rows4, _ = exchanged.shape
    rows = rows4 // 4
    seq = devs * rows
    width = slots.shape[1] * BLK
    smem = pl.BlockSpec(memory_space=pltpu.SMEM)
    vmem = pl.BlockSpec(memory_space=pltpu.VMEM)
    return pl.pallas_call(
        forward_kernel,
        out_shape=[
            jax.ShapeDtypeStruct((devs, rows, width), jnp.bfloat16),
            jax.ShapeDtypeStruct((globs.shape[0] * BLK, seq), jnp.bfloat16),
            jax.ShapeDtypeStruct((devs, rows, HDIM), jnp.bfloat16),
            jax.ShapeDtypeStruct((devs, 2, seq), jnp.float32),
        ],
        in_specs=[smem, smem, smem, vmem, vmem, vmem],
        out_specs=[vmem] * 4,
        scratch_shapes=[
            pltpu.VMEM((GROUP, rows, width), jnp.float32),
            pltpu.VMEM((globs.shape[0] * BLK, seq), jnp.float32),
        ],
        compiler_params=pltpu.CompilerParams(vmem_limit_bytes=VMEM_LIMIT),
        name="forward",
    )(slots, globs, local, exchanged, bias, gain_row)


def backward_kernel(
    slots_ref, globs_ref, in_ref, probs_ref, dense_ref, attn_ref, stat_ref, gain_ref,
    out_ref, gain_out_ref,
    low_ref, acc_ref, stage_ref, sem,
):
    devs, rows4, _ = in_ref.shape
    rows = rows4 // 4
    seq = devs * rows
    count = slots_ref.shape[1]
    globs = globs_ref.shape[0]

    stats = stat_ref[0]
    for d in range(1, devs):
        stats = stats + stat_ref[d]
    stats = stats * (1.0 / (devs * HDIM))
    inv_rms = lax.rsqrt(stats[0:1] + EPSILON)
    shrink = inv_rms * inv_rms * stats[1:2]
    gain = jnp.zeros((8, HDIM), jnp.float32)
    for i in range(devs):
        span = slice(i * rows, (i + 1) * rows)
        factor = jnp.broadcast_to(inv_rms[:, span], (HDIM, rows)).T
        minus = jnp.broadcast_to(shrink[:, span], (HDIM, rows)).T
        attn = attn_ref[i].astype(jnp.float32)
        grad = in_ref[i, 3 * rows:4 * rows, :].astype(jnp.float32)
        low_ref[i] = (factor * (gain_ref[...] * grad - attn * minus)).astype(jnp.bfloat16)
        gain = gain + jnp.sum((grad * attn * factor).reshape(rows // 8, 8, HDIM), axis=0)
    gain_out_ref[...] = jnp.sum(gain, axis=0, keepdims=True)

    def block_of(ref, block, slot):
        return block_rows(ref, block, slot, rows)

    def side(low, q):
        zero = jnp.zeros_like(low)
        return jnp.concatenate(
            [jnp.concatenate([low, zero], axis=1), jnp.concatenate([zero, q], axis=1)], axis=0
        )

    def row_dot(low, attn):
        return jnp.sum(low.astype(jnp.float32) * attn.astype(jnp.float32), axis=1, keepdims=True)

    blocks = [globs_ref[t] for t in range(globs)]
    q = jnp.concatenate([block_of(in_ref, b, 0) for b in blocks], axis=0)
    low = jnp.concatenate([block_of(low_ref, b, 0) for b in blocks], axis=0)
    attn = jnp.concatenate([block_of(attn_ref, b, 0) for b in blocks], axis=0)
    both = side(low, q)
    dots = row_dot(low, attn)
    step = 512
    dq_dense = jnp.zeros((globs * BLK, HDIM), jnp.float32)
    for c in range(seq // step):
        values = in_ref[c * 4:(c + 1) * 4, 2 * rows:3 * rows, :].reshape(step, HDIM)
        keys = in_ref[c * 4:(c + 1) * 4, rows:2 * rows, :].reshape(step, HDIM)
        probs = dense_ref[:, c * step:(c + 1) * step]
        ds = (probs.astype(jnp.float32) * (dot(low, values, NT) - dots)).astype(jnp.bfloat16)
        dq_dense = dq_dense + dot(ds, keys)
        acc_ref[c * step:(c + 1) * step, :] = dot(jnp.concatenate([probs, ds], axis=0), both, TN)

    def group(step, carry):
        results = []
        for u in range(GROUP):
            pair = step * GROUP + u
            ids = [slots_ref[pair, t] for t in range(count)]
            values = jnp.concatenate([block_of(in_ref, b, 2) for b in ids], axis=0)
            keys = jnp.concatenate([block_of(in_ref, b, 1) for b in ids], axis=0)
            q = in_ref[pair, 0:rows, :]
            low = low_ref[pair]
            probs = probs_ref[pair]
            dots = row_dot(low, attn_ref[pair])
            ds = (probs.astype(jnp.float32) * (dot(low, values, NT) - dots)).astype(jnp.bfloat16)
            stage_ref[pair, 0:rows, :] = (dot(ds, keys) * SCALE).astype(jnp.bfloat16)
            results.append((ids, dot(jnp.concatenate([probs, ds], axis=0), side(low, q), TN)))
        for ids, both in results:
            for t, block in enumerate(ids):
                acc_ref[pl.ds(pl.multiple_of(block * BLK, BLK), BLK), :] += (
                    both[t * BLK:(t + 1) * BLK]
                )
        return carry

    lax.fori_loop(0, devs // GROUP, group, 0)

    per = rows // BLK
    dq_dense = (dq_dense * SCALE).astype(jnp.bfloat16)
    for t, block in enumerate(blocks):
        stage_ref[block // per, pl.ds(pl.multiple_of((block % per) * BLK, BLK), BLK), :] = (
            dq_dense[t * BLK:(t + 1) * BLK]
        )
    for i in range(devs):
        span = slice(i * rows, (i + 1) * rows)
        stage_ref[i, rows:2 * rows, :] = (acc_ref[span, HDIM:] * SCALE).astype(jnp.bfloat16)
        stage_ref[i, 2 * rows:3 * rows, :] = acc_ref[span, :HDIM].astype(jnp.bfloat16)
    copy = pltpu.make_async_copy(stage_ref, out_ref, sem)
    copy.start()
    copy.wait()


def backward(slots, globs, exchanged, probs, dense, attn, stats, gain_row):
    devs, rows4, _ = exchanged.shape
    rows = rows4 // 4
    seq = devs * rows
    smem = pl.BlockSpec(memory_space=pltpu.SMEM)
    vmem = pl.BlockSpec(memory_space=pltpu.VMEM)
    return pl.pallas_call(
        backward_kernel,
        out_shape=[
            jax.ShapeDtypeStruct((devs, 3 * rows, HDIM), jnp.bfloat16),
            jax.ShapeDtypeStruct((1, HDIM), jnp.float32),
        ],
        in_specs=[smem, smem] + [vmem] * 6,
        out_specs=[pl.BlockSpec(memory_space=pltpu.HBM), vmem],
        scratch_shapes=[
            pltpu.VMEM((devs, rows, HDIM), jnp.bfloat16),
            pltpu.VMEM((seq, 2 * HDIM), jnp.float32),
            pltpu.VMEM((devs, 3 * rows, HDIM), jnp.bfloat16),
            pltpu.SemaphoreType.DMA,
        ],
        compiler_params=pltpu.CompilerParams(vmem_limit_bytes=VMEM_LIMIT),
        name="backward",
    )(slots, globs, exchanged, probs, dense, attn, stats, gain_row)


def pair_slots(head_width, filing_globals, head_random, count):
    pairs = count // PAIR
    first = jnp.arange(pairs, dtype=jnp.int32)[:, None] * PAIR
    near = first + jnp.arange(-WMAX, PAIR + WMAX, dtype=jnp.int32)[None, :]
    globs = jnp.broadcast_to(filing_globals[None, :], (pairs, filing_globals.shape[0]))
    rand = head_random.reshape(pairs, -1)
    ids = jnp.concatenate([near, globs, rand], axis=1)
    total = ids.shape[1]
    inside = (ids >= 0) & (ids < count)
    earlier = jnp.arange(total)[:, None] > jnp.arange(total)[None, :]
    again = jnp.any((ids[:, :, None] == ids[:, None, :]) & earlier[None], axis=2)
    live = inside & jnp.logical_not(again)
    queries = first + jnp.arange(PAIR, dtype=jnp.int32)[None, :]
    per_query = head_random.reshape(pairs, PAIR, 1, -1)
    keys = ids[:, None, :]
    allowed = (
        (jnp.abs(keys - queries[:, :, None]) <= head_width)
        | jnp.any(keys[..., None] == filing_globals, axis=-1)
        | jnp.any(keys[..., None] == per_query, axis=-1)
    )
    bias = jnp.where(allowed & live[:, None, :], 0.0, NEG_FILL).astype(jnp.float32)
    bias = jnp.repeat(bias, BLK, axis=2)
    is_global = jnp.any(queries[..., None] == filing_globals, axis=-1)
    local = jnp.where(is_global, 0.0, 1.0).astype(jnp.float32)
    return jnp.clip(ids, 0, count - 1), bias, local


def body(
    query_rows, key_rows, value_rows, out_grad, norm_gains, window, global_blocks, random_blocks
):
    seq_count = lax.axis_size("seq")
    own_count = lax.axis_size("own")
    rows = query_rows.shape[1]
    seq = rows * seq_count
    gain_scale = (own_count * seq) ** (-0.5)
    exchange = functools.partial(
        lax.all_to_all, axis_name="seq", split_axis=0, concat_axis=0, tiled=True
    )
    exchanged = exchange(pack(query_rows, key_rows, value_rows, out_grad))
    swap = [(o * own_count + s, s * own_count + o) for s in range(seq_count) for o in range(own_count)]
    gain_row = lax.ppermute(norm_gains, ("seq", "own"), swap).reshape(1, -1)
    globs = global_blocks[0]
    slots, bias, local = pair_slots(window[0], globs, random_blocks[0], seq // BLK)
    probs, dense, attn, stats = forward(slots, globs, local, exchanged, bias, gain_row)
    stats = exchange(stats)
    grads, gain_part = backward(slots, globs, exchanged, probs, dense, attn, stats, gain_row)
    gain_terms = lax.all_gather(gain_part.reshape(-1), "own")
    gain_grad = jnp.sum(gain_terms, axis=0) * gain_scale
    out_query, out_key, out_value = unpack(exchange(grads))
    return (out_query, out_key, out_value, gain_grad)


def solution(mesh):
    rows = P("own", "seq", None)
    placed = (rows, rows, rows, rows, P("own"), P("seq"), P("own", None), P("seq", None, None))
    return jax.shard_map(
        body,
        mesh=mesh,
        in_specs=placed,
        out_specs=(rows, rows, rows, P("seq")),
        check_vma=False,
    )
```

```python
import functools
import math

import jax
import jax.numpy as jnp
from jax import lax
from jax.experimental import pallas as pl
from jax.experimental.pallas import tpu as pltpu
from jax.sharding import PartitionSpec as P

HDIM = 128
BLK = 64
WMAX = 2
PAIR = 2
GROUP = 8
NEG_FILL = -1e30
EPSILON = 1e-05
SCALE = 1.0 / math.sqrt(HDIM)
EXP_FACTOR = math.log2(math.e) * SCALE
VMEM_LIMIT = 40 * 1024 * 1024
UNPACK_VMEM_LIMIT = 16 * 1024 * 1024

NT = (((1,), (1,)), ((), ()))
TN = (((0,), (0,)), ((), ()))


def dot(a, b, dims=None):
    if dims is None:
        return jnp.dot(a, b, preferred_element_type=jnp.float32)
    return lax.dot_general(a, b, dims, preferred_element_type=jnp.float32)


def pack_kernel(q_ref, k_ref, v_ref, g_ref, out_ref, stage_ref, in_sems, out_sems):
    heads = out_ref.shape[0]
    rows = q_ref.shape[1]
    loads = [
        [
            pltpu.make_async_copy(
                ref.at[0, :, h * HDIM:(h + 1) * HDIM],
                stage_ref.at[h, slot * rows:(slot + 1) * rows, :],
                in_sems.at[h, slot],
            )
            for slot, ref in enumerate((q_ref, k_ref, v_ref, g_ref))
        ]
        for h in range(heads)
    ]
    stores = [
        pltpu.make_async_copy(stage_ref.at[h], out_ref.at[h], out_sems.at[h]) for h in range(heads)
    ]
    for head_loads in loads:
        for copy in head_loads:
            copy.start()
    for head_loads, store in zip(loads, stores):
        for copy in head_loads:
            copy.wait()
        store.start()
    for store in stores:
        store.wait()


def pack(query_rows, key_rows, value_rows, out_grad):
    _, rows, cols = query_rows.shape
    heads = cols // HDIM
    return pl.pallas_call(
        pack_kernel,
        out_shape=jax.ShapeDtypeStruct((heads, 4 * rows, HDIM), query_rows.dtype),
        in_specs=[pl.BlockSpec(memory_space=pltpu.HBM)] * 4,
        out_specs=pl.BlockSpec(memory_space=pltpu.HBM),
        scratch_shapes=[
            pltpu.VMEM((heads, 4 * rows, HDIM), query_rows.dtype),
            pltpu.SemaphoreType.DMA((heads, 4)),
            pltpu.SemaphoreType.DMA((heads,)),
        ],
        name="pack",
    )(query_rows, key_rows, value_rows, out_grad)


def unpack_kernel(in_ref, q_ref, k_ref, v_ref, sems):
    heads = in_ref.shape[0]
    rows = q_ref.shape[1]
    copies = [
        pltpu.make_async_copy(
            in_ref.at[h, slot * rows:(slot + 1) * rows, :],
            ref.at[0, :, h * HDIM:(h + 1) * HDIM],
            sems.at[slot, h],
        )
        for slot, ref in enumerate((q_ref, k_ref, v_ref))
        for h in range(heads)
    ]
    for copy in copies:
        copy.start()
    for copy in copies:
        copy.wait()


def unpack(exchanged):
    heads, rows3, _ = exchanged.shape
    rows = rows3 // 3
    shape = jax.ShapeDtypeStruct((1, rows, heads * HDIM), exchanged.dtype)
    return pl.pallas_call(
        unpack_kernel,
        out_shape=[shape] * 3,
        in_specs=[pl.BlockSpec(memory_space=pltpu.VMEM)],
        out_specs=[pl.BlockSpec(memory_space=pltpu.HBM)] * 3,
        scratch_shapes=[pltpu.SemaphoreType.DMA((3, heads))],
        compiler_params=pltpu.CompilerParams(vmem_limit_bytes=UNPACK_VMEM_LIMIT),
        name="unpack",
    )(exchanged)


def block_rows(ref, block, slot, rows):
    per = rows // BLK
    offset = pl.multiple_of(slot * rows + (block % per) * BLK, BLK)
    return ref[block // per, pl.ds(offset, BLK), :]


def all_rows(ref, slot, rows):
    return ref[:, slot * rows:(slot + 1) * rows, :].reshape(ref.shape[0] * rows, HDIM)


def forward_kernel(
    slots_ref, globs_ref, local_ref, in_ref, bias_ref, gain_ref,
    probs_ref, dense_ref, attn_ref, stat_ref,
    s_ref, sd_ref,
):
    devs, rows4, _ = in_ref.shape
    rows = rows4 // 4
    count = slots_ref.shape[1]
    globs = globs_ref.shape[0]
    width = count * BLK
    seq = devs * rows

    def gather(pair, slot):
        return jnp.concatenate(
            [block_rows(in_ref, slots_ref[pair, t], slot, rows) for t in range(count)], axis=0
        )

    def group(step, carry):
        pairs = [step * GROUP + u for u in range(GROUP)]
        tops = []
        for u, pair in enumerate(pairs):
            q = in_ref[pair, 0:rows, :]
            s = dot(q, gather(pair, 1), NT)
            s = jnp.concatenate(
                [s[b * BLK:(b + 1) * BLK] + bias_ref[pair, b:b + 1, :] for b in range(PAIR)], axis=0
            )
            s_ref[u] = s
            tops.append(jnp.max(s, axis=1, keepdims=True))
        sums = []
        for u, pair in enumerate(pairs):
            e = jnp.exp2((s_ref[u] - tops[u]) * EXP_FACTOR)
            s_ref[u] = e
            sums.append(jnp.sum(e, axis=1, keepdims=True))
        for u, pair in enumerate(pairs):
            row = lax.broadcasted_iota(jnp.int32, (rows, 1), 0)
            local = jnp.where(row < BLK, local_ref[pair, 0], local_ref[pair, 1])
            probs = (s_ref[u] * (local / sums[u])).astype(jnp.bfloat16)
            probs_ref[pair] = probs
            attn_ref[pair] = dot(probs, gather(pair, 2)).astype(jnp.bfloat16)
        return carry

    lax.fori_loop(0, devs // GROUP, group, 0)

    q = jnp.concatenate([block_rows(in_ref, globs_ref[t], 0, rows) for t in range(globs)], axis=0)
    step = 512
    tops = []
    for c in range(seq // step):
        keys = in_ref[c * 4:(c + 1) * 4, rows:2 * rows, :].reshape(step, HDIM)
        s = dot(q, keys, NT)
        sd_ref[:, c * step:(c + 1) * step] = s
        tops.append(jnp.max(s, axis=1, keepdims=True))
    top = functools.reduce(jnp.maximum, tops)
    total = jnp.zeros((globs * BLK, 1), jnp.float32)
    for c in range(seq // step):
        e = jnp.exp2((sd_ref[:, c * step:(c + 1) * step] - top) * EXP_FACTOR)
        sd_ref[:, c * step:(c + 1) * step] = e
        total = total + jnp.sum(e, axis=1, keepdims=True)
    inv = 1.0 / total
    for c in range(seq // step):
        dense_ref[:, c * step:(c + 1) * step] = (
            sd_ref[:, c * step:(c + 1) * step] * inv
        ).astype(jnp.bfloat16)
    out = dot(dense_ref[...], all_rows(in_ref, 2, rows)).astype(jnp.bfloat16)
    per = rows // BLK
    for t in range(globs):
        block = globs_ref[t]
        attn_ref[block // per, pl.ds(pl.multiple_of((block % per) * BLK, BLK), BLK), :] = (
            out[t * BLK:(t + 1) * BLK]
        )

    for i in range(devs):
        attn = attn_ref[i].astype(jnp.float32)
        grad = in_ref[i, 3 * rows:4 * rows, :].astype(jnp.float32) * gain_ref[...]
        square = jnp.sum((attn * attn).T, axis=0, keepdims=True)
        inner = jnp.sum((grad * attn).T, axis=0, keepdims=True)
        stats = jnp.concatenate([square, inner], axis=0)
        for d in range(devs):
            stat_ref[d, :, i * rows:(i + 1) * rows] = stats


def forward(slots, globs, local, exchanged, bias, gain_row):
    devs, rows4, _ = exchanged.shape
    rows = rows4 // 4
    seq = devs * rows
    width = slots.shape[1] * BLK
    smem = pl.BlockSpec(memory_space=pltpu.SMEM)
    vmem = pl.BlockSpec(memory_space=pltpu.VMEM)
    return pl.pallas_call(
        forward_kernel,
        out_shape=[
            jax.ShapeDtypeStruct((devs, rows, width), jnp.bfloat16),
            jax.ShapeDtypeStruct((globs.shape[0] * BLK, seq), jnp.bfloat16),
            jax.ShapeDtypeStruct((devs, rows, HDIM), jnp.bfloat16),
            jax.ShapeDtypeStruct((devs, 2, seq), jnp.float32),
        ],
        in_specs=[smem, smem, smem, vmem, vmem, vmem],
        out_specs=[vmem] * 4,
        scratch_shapes=[
            pltpu.VMEM((GROUP, rows, width), jnp.float32),
            pltpu.VMEM((globs.shape[0] * BLK, seq), jnp.float32),
        ],
        compiler_params=pltpu.CompilerParams(vmem_limit_bytes=VMEM_LIMIT),
        name="forward",
    )(slots, globs, local, exchanged, bias, gain_row)


def backward_kernel(
    slots_ref, globs_ref, in_ref, probs_ref, dense_ref, attn_ref, stat_ref, gain_ref,
    out_ref, gain_out_ref,
    low_ref, acc_ref, stage_ref, sem,
):
    devs, rows4, _ = in_ref.shape
    rows = rows4 // 4
    seq = devs * rows
    count = slots_ref.shape[1]
    globs = globs_ref.shape[0]

    stats = stat_ref[0]
    for d in range(1, devs):
        stats = stats + stat_ref[d]
    stats = stats * (1.0 / (devs * HDIM))
    inv_rms = lax.rsqrt(stats[0:1] + EPSILON)
    shrink = inv_rms * inv_rms * stats[1:2]
    gain = jnp.zeros((8, HDIM), jnp.float32)
    for i in range(devs):
        span = slice(i * rows, (i + 1) * rows)
        factor = jnp.broadcast_to(inv_rms[:, span], (HDIM, rows)).T
        minus = jnp.broadcast_to(shrink[:, span], (HDIM, rows)).T
        attn = attn_ref[i].astype(jnp.float32)
        grad = in_ref[i, 3 * rows:4 * rows, :].astype(jnp.float32)
        low_ref[i] = (factor * (gain_ref[...] * grad - attn * minus)).astype(jnp.bfloat16)
        gain = gain + jnp.sum((grad * attn * factor).reshape(rows // 8, 8, HDIM), axis=0)
    gain_out_ref[...] = jnp.sum(gain, axis=0, keepdims=True)

    def block_of(ref, block, slot):
        return block_rows(ref, block, slot, rows)

    def side(low, q):
        zero = jnp.zeros_like(low)
        return jnp.concatenate(
            [jnp.concatenate([low, zero], axis=1), jnp.concatenate([zero, q], axis=1)], axis=0
        )

    def row_dot(low, attn):
        return jnp.sum(low.astype(jnp.float32) * attn.astype(jnp.float32), axis=1, keepdims=True)

    blocks = [globs_ref[t] for t in range(globs)]
    q = jnp.concatenate([block_of(in_ref, b, 0) for b in blocks], axis=0)
    low = jnp.concatenate([block_of(low_ref, b, 0) for b in blocks], axis=0)
    attn = jnp.concatenate([block_of(attn_ref, b, 0) for b in blocks], axis=0)
    both = side(low, q)
    dots = row_dot(low, attn)
    step = 512
    dq_dense = jnp.zeros((globs * BLK, HDIM), jnp.float32)
    for c in range(seq // step):
        values = in_ref[c * 4:(c + 1) * 4, 2 * rows:3 * rows, :].reshape(step, HDIM)
        keys = in_ref[c * 4:(c + 1) * 4, rows:2 * rows, :].reshape(step, HDIM)
        probs = dense_ref[:, c * step:(c + 1) * step]
        ds = (probs.astype(jnp.float32) * (dot(low, values, NT) - dots)).astype(jnp.bfloat16)
        dq_dense = dq_dense + dot(ds, keys)
        acc_ref[c * step:(c + 1) * step, :] = dot(jnp.concatenate([probs, ds], axis=0), both, TN)

    def group(step, carry):
        results = []
        for u in range(GROUP):
            pair = step * GROUP + u
            ids = [slots_ref[pair, t] for t in range(count)]
            values = jnp.concatenate([block_of(in_ref, b, 2) for b in ids], axis=0)
            keys = jnp.concatenate([block_of(in_ref, b, 1) for b in ids], axis=0)
            q = in_ref[pair, 0:rows, :]
            low = low_ref[pair]
            probs = probs_ref[pair]
            dots = row_dot(low, attn_ref[pair])
            ds = (probs.astype(jnp.float32) * (dot(low, values, NT) - dots)).astype(jnp.bfloat16)
            stage_ref[pair, 0:rows, :] = (dot(ds, keys) * SCALE).astype(jnp.bfloat16)
            results.append((ids, dot(jnp.concatenate([probs, ds], axis=0), side(low, q), TN)))
        for ids, both in results:
            for t, block in enumerate(ids):
                acc_ref[pl.ds(pl.multiple_of(block * BLK, BLK), BLK), :] += (
                    both[t * BLK:(t + 1) * BLK]
                )
        return carry

    lax.fori_loop(0, devs // GROUP, group, 0)

    per = rows // BLK
    dq_dense = (dq_dense * SCALE).astype(jnp.bfloat16)
    for t, block in enumerate(blocks):
        stage_ref[block // per, pl.ds(pl.multiple_of((block % per) * BLK, BLK), BLK), :] = (
            dq_dense[t * BLK:(t + 1) * BLK]
        )
    for i in range(devs):
        span = slice(i * rows, (i + 1) * rows)
        stage_ref[i, rows:2 * rows, :] = (acc_ref[span, HDIM:] * SCALE).astype(jnp.bfloat16)
        stage_ref[i, 2 * rows:3 * rows, :] = acc_ref[span, :HDIM].astype(jnp.bfloat16)
    copy = pltpu.make_async_copy(stage_ref, out_ref, sem)
    copy.start()
    copy.wait()


def backward(slots, globs, exchanged, probs, dense, attn, stats, gain_row):
    devs, rows4, _ = exchanged.shape
    rows = rows4 // 4
    seq = devs * rows
    smem = pl.BlockSpec(memory_space=pltpu.SMEM)
    vmem = pl.BlockSpec(memory_space=pltpu.VMEM)
    return pl.pallas_call(
        backward_kernel,
        out_shape=[
            pltpu.HBM((devs, 3 * rows, HDIM), jnp.bfloat16),
            jax.ShapeDtypeStruct((1, HDIM), jnp.float32),
        ],
        in_specs=[smem, smem] + [vmem] * 6,
        out_specs=[pl.BlockSpec(memory_space=pltpu.HBM), vmem],
        scratch_shapes=[
            pltpu.VMEM((devs, rows, HDIM), jnp.bfloat16),
            pltpu.VMEM((seq, 2 * HDIM), jnp.float32),
            pltpu.VMEM((devs, 3 * rows, HDIM), jnp.bfloat16),
            pltpu.SemaphoreType.DMA,
        ],
        compiler_params=pltpu.CompilerParams(vmem_limit_bytes=VMEM_LIMIT),
        name="backward",
    )(slots, globs, exchanged, probs, dense, attn, stats, gain_row)


def pair_slots(head_width, filing_globals, head_random, count):
    pairs = count // PAIR
    first = jnp.arange(pairs, dtype=jnp.int32)[:, None] * PAIR
    near = first + jnp.arange(-WMAX, PAIR + WMAX, dtype=jnp.int32)[None, :]
    globs = jnp.broadcast_to(filing_globals[None, :], (pairs, filing_globals.shape[0]))
    rand = head_random.reshape(pairs, -1)
    ids = jnp.concatenate([near, globs, rand], axis=1)
    total = ids.shape[1]
    inside = (ids >= 0) & (ids < count)
    earlier = jnp.arange(total)[:, None] > jnp.arange(total)[None, :]
    again = jnp.any((ids[:, :, None] == ids[:, None, :]) & earlier[None], axis=2)
    live = inside & jnp.logical_not(again)
    queries = first + jnp.arange(PAIR, dtype=jnp.int32)[None, :]
    per_query = head_random.reshape(pairs, PAIR, 1, -1)
    keys = ids[:, None, :]
    allowed = (
        (jnp.abs(keys - queries[:, :, None]) <= head_width)
        | jnp.any(keys[..., None] == filing_globals, axis=-1)
        | jnp.any(keys[..., None] == per_query, axis=-1)
    )
    bias = jnp.where(allowed & live[:, None, :], 0.0, NEG_FILL).astype(jnp.float32)
    bias = jnp.repeat(bias, BLK, axis=2)
    is_global = jnp.any(queries[..., None] == filing_globals, axis=-1)
    local = jnp.where(is_global, 0.0, 1.0).astype(jnp.float32)
    return jnp.clip(ids, 0, count - 1), bias, local


def body(
    query_rows, key_rows, value_rows, out_grad, norm_gains, window, global_blocks, random_blocks
):
    seq_count = lax.axis_size("seq")
    own_count = lax.axis_size("own")
    rows = query_rows.shape[1]
    seq = rows * seq_count
    gain_scale = (own_count * seq) ** (-0.5)
    exchange = functools.partial(
        lax.all_to_all, axis_name="seq", split_axis=0, concat_axis=0, tiled=True
    )
    exchanged = exchange(pack(query_rows, key_rows, value_rows, out_grad))
    gains = lax.all_gather(norm_gains, "own")
    gain_row = lax.dynamic_slice_in_dim(gains, lax.axis_index("seq"), 1, axis=0)
    globs = global_blocks[0]
    slots, bias, local = pair_slots(window[0], globs, random_blocks[0], seq // BLK)
    probs, dense, attn, stats = forward(slots, globs, local, exchanged, bias, gain_row)
    stats = exchange(stats)
    grads, gain_part = backward(slots, globs, exchanged, probs, dense, attn, stats, gain_row)
    gain_terms = lax.all_gather(gain_part.reshape(-1), "own")
    gain_grad = jnp.sum(gain_terms, axis=0) * gain_scale
    out_query, out_key, out_value = unpack(exchange(grads))
    return (out_query, out_key, out_value, gain_grad)


def solution(mesh):
    rows = P("own", "seq", None)
    placed = (rows, rows, rows, rows, P("own"), P("seq"), P("own", None), P("seq", None, None))
    return jax.shard_map(
        body,
        mesh=mesh,
        in_specs=placed,
        out_specs=(rows, rows, rows, P("seq")),
        check_vma=False,
    )
```

```python
import functools
import math

import jax
import jax.numpy as jnp
from jax import lax
from jax.experimental import pallas as pl
from jax.experimental.pallas import tpu as pltpu
from jax.sharding import PartitionSpec as P

HDIM = 128
BLK = 64
WMAX = 2
PAIR = 2
GLOB = 2
GLOB_AT = PAIR + 2 * WMAX
GROUP = 16
NEG_FILL = -1e30
EPSILON = 1e-05
SCALE = 1.0 / math.sqrt(HDIM)
EXP_FACTOR = math.log2(math.e) * SCALE
VMEM_LIMIT = 40 * 1024 * 1024
SUM_LOW = 2.0 ** -80
SUM_HIGH = 2.0 ** 80
UNPACK_VMEM_LIMIT = 16 * 1024 * 1024

NT = (((1,), (1,)), ((), ()))
TN = (((0,), (0,)), ((), ()))


def dot(a, b, dims=None):
    if dims is None:
        return jnp.dot(a, b, preferred_element_type=jnp.float32)
    return lax.dot_general(a, b, dims, preferred_element_type=jnp.float32)


def pack_kernel(q_ref, k_ref, v_ref, g_ref, out_ref, stage_ref, in_sems, out_sems):
    heads = out_ref.shape[0]
    rows = q_ref.shape[1]
    loads = [
        [
            pltpu.make_async_copy(
                ref.at[0, :, h * HDIM:(h + 1) * HDIM],
                stage_ref.at[h, slot * rows:(slot + 1) * rows, :],
                in_sems.at[h, slot],
            )
            for slot, ref in enumerate((q_ref, k_ref, v_ref, g_ref))
        ]
        for h in range(heads)
    ]
    stores = [
        pltpu.make_async_copy(stage_ref.at[h], out_ref.at[h], out_sems.at[h]) for h in range(heads)
    ]
    for head_loads in loads:
        for copy in head_loads:
            copy.start()
    for head_loads, store in zip(loads, stores):
        for copy in head_loads:
            copy.wait()
        store.start()
    for store in stores:
        store.wait()


def pack(query_rows, key_rows, value_rows, out_grad):
    _, rows, cols = query_rows.shape
    heads = cols // HDIM
    return pl.pallas_call(
        pack_kernel,
        out_shape=jax.ShapeDtypeStruct((heads, 4 * rows, HDIM), query_rows.dtype),
        in_specs=[pl.BlockSpec(memory_space=pltpu.HBM)] * 4,
        out_specs=pl.BlockSpec(memory_space=pltpu.HBM),
        scratch_shapes=[
            pltpu.VMEM((heads, 4 * rows, HDIM), query_rows.dtype),
            pltpu.SemaphoreType.DMA((heads, 4)),
            pltpu.SemaphoreType.DMA((heads,)),
        ],
        name="pack",
    )(query_rows, key_rows, value_rows, out_grad)


def unpack_kernel(in_ref, q_ref, k_ref, v_ref, sems):
    heads = in_ref.shape[0]
    rows = q_ref.shape[1]
    copies = [
        pltpu.make_async_copy(
            in_ref.at[h, slot * rows:(slot + 1) * rows, :],
            ref.at[0, :, h * HDIM:(h + 1) * HDIM],
            sems.at[slot, h],
        )
        for slot, ref in enumerate((q_ref, k_ref, v_ref))
        for h in range(heads)
    ]
    for copy in copies:
        copy.start()
    for copy in copies:
        copy.wait()


def unpack(exchanged):
    heads, rows3, _ = exchanged.shape
    rows = rows3 // 3
    shape = jax.ShapeDtypeStruct((1, rows, heads * HDIM), exchanged.dtype)
    return pl.pallas_call(
        unpack_kernel,
        out_shape=[shape] * 3,
        in_specs=[pl.BlockSpec(memory_space=pltpu.VMEM)],
        out_specs=[pl.BlockSpec(memory_space=pltpu.HBM)] * 3,
        scratch_shapes=[pltpu.SemaphoreType.DMA((3, heads))],
        compiler_params=pltpu.CompilerParams(vmem_limit_bytes=UNPACK_VMEM_LIMIT),
        name="unpack",
    )(exchanged)


def block_rows(ref, block, slot, rows):
    per = rows // BLK
    offset = pl.multiple_of(slot * rows + (block % per) * BLK, BLK)
    return ref[block // per, pl.ds(offset, BLK), :]


def all_rows(ref, slot, rows):
    return ref[:, slot * rows:(slot + 1) * rows, :].reshape(ref.shape[0] * rows, HDIM)


def forward_kernel(
    slots_ref, in_ref, bias_ref, gain_ref,
    probs_ref, dense_ref, attn_ref, inv_ref, inv_dense_ref, stat_ref,
    low_ref, high_ref,
):
    devs, rows4, _ = in_ref.shape
    rows = rows4 // 4
    count = slots_ref.shape[1]
    globs = GLOB
    glob_ids = [slots_ref[0, GLOB_AT + t] for t in range(globs)]
    per = rows // BLK

    def gather(pair, slot):
        return jnp.concatenate(
            [block_rows(in_ref, slots_ref[pair, t], slot, rows) for t in range(count)], axis=0
        )

    def pair_pass(pair, exact):
        s = dot(in_ref[pair, 0:rows, :], gather(pair, 1), NT)
        bias = bias_ref[pair]
        if exact:
            s = jnp.concatenate(
                [s[b * BLK:(b + 1) * BLK] + bias[b:b + 1] for b in range(PAIR)], axis=0
            )
            e = jnp.exp2((s - jnp.max(s, axis=1, keepdims=True)) * EXP_FACTOR)
        else:
            e = jnp.concatenate(
                [
                    jnp.exp2(s[b * BLK:(b + 1) * BLK] * EXP_FACTOR + bias[b:b + 1])
                    for b in range(PAIR)
                ],
                axis=0,
            )
        e = e.astype(jnp.bfloat16)
        values = jnp.concatenate(
            [gather(pair, 2), jnp.ones((count * BLK, HDIM), jnp.bfloat16)], axis=1
        )
        out = dot(e, values)
        total = out[:, HDIM:]
        row = lax.broadcasted_iota(jnp.int32, (rows, HDIM), 0)
        local = []
        for b in range(PAIR):
            is_global = functools.reduce(
                jnp.logical_or, [pair * PAIR + b == block for block in glob_ids]
            )
            local.append(jnp.where(is_global, 0.0, 1.0))
        inv = jnp.where(row < BLK, local[0], local[1]) / total
        probs_ref[pair] = e
        inv_ref[pair] = inv
        attn_ref[pair] = (out[:, :HDIM] * inv).astype(jnp.bfloat16)
        return total

    def dense_pass(exact):
        q = jnp.concatenate(
            [block_rows(in_ref, block, 0, rows) for block in glob_ids], axis=0
        )
        if exact:
            top = jnp.full((globs * BLK, 1), NEG_FILL, jnp.float32)
            for c in range(devs):
                s = dot(q, in_ref[c, rows:2 * rows, :], NT)
                top = jnp.maximum(top, jnp.max(s, axis=1, keepdims=True))
        else:
            top = 0.0
        out = jnp.zeros((globs * BLK, 2 * HDIM), jnp.float32)
        ones = jnp.ones((2 * rows, HDIM), jnp.bfloat16)
        for c in range(devs // 2):
            keys = in_ref[2 * c:2 * c + 2, rows:2 * rows, :].reshape(2 * rows, HDIM)
            values = in_ref[2 * c:2 * c + 2, 2 * rows:3 * rows, :].reshape(2 * rows, HDIM)
            e = jnp.exp2((dot(q, keys, NT) - top) * EXP_FACTOR).astype(jnp.bfloat16)
            dense_ref[:, 2 * c * rows:2 * (c + 1) * rows] = e
            out = out + dot(e, jnp.concatenate([values, ones], axis=1))
        total = out[:, HDIM:]
        inv = 1.0 / total
        inv_dense_ref[...] = inv
        out = (out[:, :HDIM] * inv).astype(jnp.bfloat16)
        for t, block in enumerate(glob_ids):
            attn_ref[block // per, pl.ds(pl.multiple_of((block % per) * BLK, BLK), BLK), :] = (
                out[t * BLK:(t + 1) * BLK]
            )
        return total

    def group(step, carry):
        totals = [pair_pass(step * GROUP + u, False) for u in range(GROUP)]
        low_ref[...] = functools.reduce(jnp.minimum, totals, low_ref[...])
        high_ref[...] = functools.reduce(jnp.maximum, totals, high_ref[...])
        return carry

    def single(pair, carry):
        pair_pass(pair, True)
        return carry

    low_ref[...] = jnp.full_like(low_ref, 1.0)
    high_ref[...] = jnp.full_like(high_ref, 1.0)
    lax.fori_loop(0, devs // GROUP, group, 0)
    total = dense_pass(False)
    low = jnp.min(jnp.minimum(low_ref[...], total))
    high = jnp.max(jnp.maximum(high_ref[...], total))
    in_range = (low > SUM_LOW) & (high < SUM_HIGH)

    @pl.when(jnp.logical_not(in_range))
    def _():
        lax.fori_loop(0, devs, single, 0)
        dense_pass(True)

    for i in range(devs):
        attn = attn_ref[i].astype(jnp.float32)
        grad = in_ref[i, 3 * rows:4 * rows, :].astype(jnp.float32) * gain_ref[...]
        square = jnp.sum((attn * attn).T, axis=0, keepdims=True)
        inner = jnp.sum((grad * attn).T, axis=0, keepdims=True)
        stats = jnp.concatenate([square, inner], axis=0)
        for d in range(devs):
            stat_ref[d, :, i * rows:(i + 1) * rows] = stats


def forward(slots, exchanged, bias, gain_row):
    devs, rows4, _ = exchanged.shape
    rows = rows4 // 4
    seq = devs * rows
    width = slots.shape[1] * BLK
    smem = pl.BlockSpec(memory_space=pltpu.SMEM)
    vmem = pl.BlockSpec(memory_space=pltpu.VMEM)
    return pl.pallas_call(
        forward_kernel,
        out_shape=[
            jax.ShapeDtypeStruct((devs, rows, width), jnp.bfloat16),
            jax.ShapeDtypeStruct((GLOB * BLK, seq), jnp.bfloat16),
            jax.ShapeDtypeStruct((devs, rows, HDIM), jnp.bfloat16),
            jax.ShapeDtypeStruct((devs, rows, HDIM), jnp.float32),
            jax.ShapeDtypeStruct((GLOB * BLK, HDIM), jnp.float32),
            jax.ShapeDtypeStruct((devs, 2, seq), jnp.float32),
        ],
        in_specs=[smem, vmem, vmem, vmem],
        out_specs=[vmem] * 6,
        scratch_shapes=[pltpu.VMEM((rows, HDIM), jnp.float32)] * 2,
        compiler_params=pltpu.CompilerParams(vmem_limit_bytes=VMEM_LIMIT),
        name="forward",
    )(slots, exchanged, bias, gain_row)


def backward_kernel(
    slots_ref, in_ref, probs_ref, dense_ref, attn_ref, inv_ref, inv_dense_ref, stat_ref,
    gain_ref,
    out_ref, gain_out_ref,
    grad_ref, acc_ref, stage_ref, sems,
):
    devs, rows4, _ = in_ref.shape
    rows = rows4 // 4
    seq = devs * rows
    count = slots_ref.shape[1]
    globs = GLOB

    stats = stat_ref[0]
    for d in range(1, devs):
        stats = stats + stat_ref[d]
    stats = stats * (1.0 / (devs * HDIM))
    inv_rms = lax.rsqrt(stats[0:1] + EPSILON)
    shrink = inv_rms * inv_rms * stats[1:2]
    gain = jnp.zeros((8, HDIM), jnp.float32)
    for i in range(devs):
        span = slice(i * rows, (i + 1) * rows)
        factor = jnp.broadcast_to(inv_rms[:, span], (HDIM, rows)).T
        minus = jnp.broadcast_to(shrink[:, span], (HDIM, rows)).T
        attn = attn_ref[i].astype(jnp.float32)
        grad = in_ref[i, 3 * rows:4 * rows, :].astype(jnp.float32)
        grad_ref[i] = factor * (gain_ref[...] * grad - attn * minus)
        gain = gain + jnp.sum((grad * attn * factor).reshape(rows // 8, 8, HDIM), axis=0)
    gain_out_ref[...] = jnp.sum(gain, axis=0, keepdims=True)

    def block_of(ref, block, slot):
        return block_rows(ref, block, slot, rows)

    def side(low, q):
        zero = jnp.zeros_like(low)
        return jnp.concatenate(
            [jnp.concatenate([low, zero], axis=1), jnp.concatenate([zero, q], axis=1)], axis=0
        )

    def row_dot(low, attn):
        return jnp.sum(low.astype(jnp.float32) * attn.astype(jnp.float32), axis=1, keepdims=True)

    blocks = [slots_ref[0, GLOB_AT + t] for t in range(globs)]
    q = jnp.concatenate([block_of(in_ref, b, 0) for b in blocks], axis=0)
    low = jnp.concatenate([block_of(grad_ref, b, 0) for b in blocks], axis=0) * inv_dense_ref[...]
    low = low.astype(jnp.bfloat16)
    attn = jnp.concatenate([block_of(attn_ref, b, 0) for b in blocks], axis=0)
    both = side(low, q)
    dots = row_dot(low, attn)
    step = 512
    dq_dense = jnp.zeros((globs * BLK, HDIM), jnp.float32)
    for c in range(seq // step):
        values = in_ref[c * 4:(c + 1) * 4, 2 * rows:3 * rows, :].reshape(step, HDIM)
        keys = in_ref[c * 4:(c + 1) * 4, rows:2 * rows, :].reshape(step, HDIM)
        probs = dense_ref[:, c * step:(c + 1) * step]
        ds = (probs.astype(jnp.float32) * (dot(low, values, NT) - dots)).astype(jnp.bfloat16)
        dq_dense = dq_dense + dot(ds, keys)
        acc_ref[c * step:(c + 1) * step, :] = dot(jnp.concatenate([probs, ds], axis=0), both, TN)

    def group(step, carry):
        for u in range(GROUP):
            pair = step * GROUP + u
            ids = [slots_ref[pair, t] for t in range(count)]
            values = jnp.concatenate([block_of(in_ref, b, 2) for b in ids], axis=0)
            keys = jnp.concatenate([block_of(in_ref, b, 1) for b in ids], axis=0)
            q = in_ref[pair, 0:rows, :]
            low = (grad_ref[pair] * inv_ref[pair]).astype(jnp.bfloat16)
            probs = probs_ref[pair]
            dots = row_dot(low, attn_ref[pair])
            ds = (probs.astype(jnp.float32) * (dot(low, values, NT) - dots)).astype(jnp.bfloat16)
            stage_ref[pair, 0:rows, :] = (dot(ds, keys) * SCALE).astype(jnp.bfloat16)
            both = dot(jnp.concatenate([probs, ds], axis=0), side(low, q), TN)
            for t, block in enumerate(ids):
                acc_ref[pl.ds(pl.multiple_of(block * BLK, BLK), BLK), :] += (
                    both[t * BLK:(t + 1) * BLK]
                )
        return carry

    lax.fori_loop(0, devs // GROUP, group, 0)

    per = rows // BLK
    dq_dense = (dq_dense * SCALE).astype(jnp.bfloat16)
    for t, block in enumerate(blocks):
        stage_ref[block // per, pl.ds(pl.multiple_of((block % per) * BLK, BLK), BLK), :] = (
            dq_dense[t * BLK:(t + 1) * BLK]
        )
    copies = []
    for i in range(devs):
        span = slice(i * rows, (i + 1) * rows)
        stage_ref[i, rows:2 * rows, :] = (acc_ref[span, HDIM:] * SCALE).astype(jnp.bfloat16)
        stage_ref[i, 2 * rows:3 * rows, :] = acc_ref[span, :HDIM].astype(jnp.bfloat16)
        copies.append(pltpu.make_async_copy(stage_ref.at[i], out_ref.at[i], sems.at[i]))
        copies[-1].start()
    for copy in copies:
        copy.wait()


def backward(slots, exchanged, forwarded, stats, gain_row):
    devs, rows4, _ = exchanged.shape
    rows = rows4 // 4
    seq = devs * rows
    smem = pl.BlockSpec(memory_space=pltpu.SMEM)
    vmem = pl.BlockSpec(memory_space=pltpu.VMEM)
    return pl.pallas_call(
        backward_kernel,
        out_shape=[
            pltpu.HBM((devs, 3 * rows, HDIM), jnp.bfloat16),
            jax.ShapeDtypeStruct((1, HDIM), jnp.float32),
        ],
        in_specs=[smem] + [vmem] * 8,
        out_specs=[pl.BlockSpec(memory_space=pltpu.HBM), vmem],
        scratch_shapes=[
            pltpu.VMEM((devs, rows, HDIM), jnp.float32),
            pltpu.VMEM((seq, 2 * HDIM), jnp.float32),
            pltpu.VMEM((devs, 3 * rows, HDIM), jnp.bfloat16),
            pltpu.SemaphoreType.DMA((devs,)),
        ],
        compiler_params=pltpu.CompilerParams(vmem_limit_bytes=VMEM_LIMIT),
        name="backward",
    )(slots, exchanged, *forwarded, stats, gain_row)


def pair_slots(head_width, filing_globals, head_random, count):
    pairs = count // PAIR
    first = jnp.arange(pairs, dtype=jnp.int32)[:, None] * PAIR
    near = first + jnp.arange(-WMAX, PAIR + WMAX, dtype=jnp.int32)[None, :]
    globs = jnp.broadcast_to(filing_globals[None, :], (pairs, filing_globals.shape[0]))
    rand = head_random.reshape(pairs, -1)
    ids = jnp.concatenate([near, globs, rand], axis=1)
    total = ids.shape[1]
    inside = (ids >= 0) & (ids < count)
    earlier = jnp.arange(total)[:, None] > jnp.arange(total)[None, :]
    again = jnp.any((ids[:, :, None] == ids[:, None, :]) & earlier[None], axis=2)
    live = inside & jnp.logical_not(again)
    queries = first + jnp.arange(PAIR, dtype=jnp.int32)[None, :]
    per_query = head_random.reshape(pairs, PAIR, 1, -1)
    keys = ids[:, None, :]
    allowed = (
        (jnp.abs(keys - queries[:, :, None]) <= head_width)
        | jnp.any(keys[..., None] == filing_globals, axis=-1)
        | jnp.any(keys[..., None] == per_query, axis=-1)
    )
    bias = jnp.where(allowed & live[:, None, :], 0.0, NEG_FILL).astype(jnp.float32)
    bias = jnp.repeat(bias, BLK, axis=2)
    return jnp.clip(ids, 0, count - 1), bias


def body(
    query_rows, key_rows, value_rows, out_grad, norm_gains, window, global_blocks, random_blocks
):
    seq_count = lax.axis_size("seq")
    own_count = lax.axis_size("own")
    rows = query_rows.shape[1]
    seq = rows * seq_count
    gain_scale = (own_count * seq) ** (-0.5)
    exchange = functools.partial(
        lax.all_to_all, axis_name="seq", split_axis=0, concat_axis=0, tiled=True
    )
    exchanged = exchange(pack(query_rows, key_rows, value_rows, out_grad))
    gains = lax.all_gather(norm_gains, "own")
    gain_row = lax.dynamic_slice_in_dim(gains, lax.axis_index("seq"), 1, axis=0)
    slots, bias = pair_slots(window[0], global_blocks[0], random_blocks[0], seq // BLK)
    *forwarded, stats = forward(slots, exchanged, bias, gain_row)
    stats = exchange(stats)
    grads, gain_part = backward(slots, exchanged, forwarded, stats, gain_row)
    gain_terms = lax.all_gather(gain_part.reshape(-1), "own")
    gain_grad = jnp.sum(gain_terms, axis=0) * gain_scale
    out_query, out_key, out_value = unpack(exchange(grads))
    return (out_query, out_key, out_value, gain_grad)


def solution(mesh):
    rows = P("own", "seq", None)
    placed = (rows, rows, rows, rows, P("own"), P("seq"), P("own", None), P("seq", None, None))
    return jax.shard_map(
        body,
        mesh=mesh,
        in_specs=placed,
        out_specs=(rows, rows, rows, P("seq")),
        check_vma=False,
    )
```

```python
import functools
import math

import jax
import jax.numpy as jnp
from jax import lax
from jax.experimental import pallas as pl
from jax.experimental.pallas import tpu as pltpu
from jax.sharding import PartitionSpec as P

HDIM = 128
BLK = 64
WMAX = 2
PAIR = 2
GLOB = 2
GLOB_AT = PAIR + 2 * WMAX
PARTS = 2
PIECES = 4
NEG_FILL = -1e30
EPSILON = 1e-05
SCALE = 1.0 / math.sqrt(HDIM)
EXP_FACTOR = math.log2(math.e) * SCALE
VMEM_LIMIT = 40 * 1024 * 1024
SUM_LOW = 2.0 ** -80
SUM_HIGH = 2.0 ** 80
COPY_VMEM_LIMIT = 16 * 1024 * 1024

NT = (((1,), (1,)), ((), ()))
TN = (((0,), (0,)), ((), ()))


def dot(a, b, dims=None):
    if dims is None:
        return jnp.dot(a, b, preferred_element_type=jnp.float32)
    return lax.dot_general(a, b, dims, preferred_element_type=jnp.float32)


def pack_kernel(q_ref, k_ref, v_ref, g_ref, out_ref, raw_ref, stage_ref, in_sems, out_sems):
    heads = out_ref.shape[0]
    rows = q_ref.shape[1]
    part = rows // PARTS
    pieces = [(slot, c) for slot in range(4) for c in range(PARTS)]
    refs = (q_ref, k_ref, v_ref, g_ref)
    loads = [
        pltpu.make_async_copy(
            refs[slot].at[0, c * part:(c + 1) * part, :],
            raw_ref.at[slot, c * part:(c + 1) * part, :],
            in_sems.at[slot, c],
        )
        for slot, c in pieces
    ]
    for copy in loads:
        copy.start()
    stores = []
    for (slot, c), copy in zip(pieces, loads):
        copy.wait()
        span = slice(slot * rows + c * part, slot * rows + (c + 1) * part)
        for h in range(heads):
            stage_ref[h, span, :] = (
                raw_ref[slot, c * part:(c + 1) * part, h * HDIM:(h + 1) * HDIM]
            )
        stores.append(
            pltpu.make_async_copy(
                stage_ref.at[:, span, :], out_ref.at[:, span, :], out_sems.at[slot, c]
            )
        )
        stores[-1].start()
    for copy in stores:
        copy.wait()


def pack(query_rows, key_rows, value_rows, out_grad):
    _, rows, cols = query_rows.shape
    heads = cols // HDIM
    dtype = query_rows.dtype
    return pl.pallas_call(
        pack_kernel,
        out_shape=pltpu.HBM((heads, 4 * rows, HDIM), dtype),
        in_specs=[pl.BlockSpec(memory_space=pltpu.HBM)] * 4,
        out_specs=pl.BlockSpec(memory_space=pltpu.HBM),
        scratch_shapes=[
            pltpu.VMEM((4, rows, cols), dtype),
            pltpu.VMEM((heads, 4 * rows, HDIM), dtype),
            pltpu.SemaphoreType.DMA((4, PARTS)),
            pltpu.SemaphoreType.DMA((4, PARTS)),
        ],
        name="pack",
    )(query_rows, key_rows, value_rows, out_grad)


def unpack_kernel(in_ref, q_ref, k_ref, v_ref, stage_ref, sems):
    heads = in_ref.shape[0]
    rows = q_ref.shape[1]
    part = rows // PARTS
    copies = []
    for slot, ref in enumerate((q_ref, k_ref, v_ref)):
        for c in range(PARTS):
            span = slice(c * part, (c + 1) * part)
            for h in range(heads):
                stage_ref[slot, span, h * HDIM:(h + 1) * HDIM] = (
                    in_ref[h, slot * rows + c * part:slot * rows + (c + 1) * part, :]
                )
            copies.append(
                pltpu.make_async_copy(
                    stage_ref.at[slot, span, :], ref.at[0, span, :], sems.at[slot, c]
                )
            )
            copies[-1].start()
    for copy in copies:
        copy.wait()


def unpack(exchanged):
    heads, rows3, _ = exchanged.shape
    rows = rows3 // 3
    shape = jax.ShapeDtypeStruct((1, rows, heads * HDIM), exchanged.dtype)
    return pl.pallas_call(
        unpack_kernel,
        out_shape=[shape] * 3,
        in_specs=[pl.BlockSpec(memory_space=pltpu.VMEM)],
        out_specs=[pl.BlockSpec(memory_space=pltpu.HBM)] * 3,
        scratch_shapes=[
            pltpu.VMEM((3, rows, heads * HDIM), exchanged.dtype),
            pltpu.SemaphoreType.DMA((3, PARTS)),
        ],
        compiler_params=pltpu.CompilerParams(vmem_limit_bytes=COPY_VMEM_LIMIT),
        name="unpack",
    )(exchanged)


def block_rows(ref, block, slot, rows):
    per = rows // BLK
    offset = pl.multiple_of(slot * rows + (block % per) * BLK, BLK)
    return ref[block // per, pl.ds(offset, BLK), :]


def all_rows(ref, slot, rows):
    return ref[:, slot * rows:(slot + 1) * rows, :].reshape(ref.shape[0] * rows, HDIM)


def forward_kernel(
    slots_ref, in_ref, bias_ref, gain_ref,
    probs_ref, dense_ref, attn_ref, inv_ref, inv_dense_ref, stat_ref,
    part_ref,
):
    devs, rows4, _ = in_ref.shape
    rows = rows4 // 4
    count = slots_ref.shape[1]
    globs = GLOB
    glob_ids = [slots_ref[0, GLOB_AT + t] for t in range(globs)]
    per = rows // BLK

    def gather(pair, slot):
        return jnp.concatenate(
            [block_rows(in_ref, slots_ref[pair, t], slot, rows) for t in range(count)], axis=0
        )

    def pair_pass(pair, exact):
        s = dot(in_ref[pair, 0:rows, :], gather(pair, 1), NT)
        bias = bias_ref[pair]
        if exact:
            s = jnp.concatenate(
                [s[b * BLK:(b + 1) * BLK] + bias[b:b + 1] for b in range(PAIR)], axis=0
            )
            e = jnp.exp2((s - jnp.max(s, axis=1, keepdims=True)) * EXP_FACTOR)
        else:
            e = jnp.concatenate(
                [
                    jnp.exp2(s[b * BLK:(b + 1) * BLK] * EXP_FACTOR + bias[b:b + 1])
                    for b in range(PAIR)
                ],
                axis=0,
            )
        e = e.astype(jnp.bfloat16)
        values = jnp.concatenate(
            [gather(pair, 2), jnp.ones((count * BLK, HDIM), jnp.bfloat16)], axis=1
        )
        out = dot(e, values)
        total = out[:, HDIM:]
        row = lax.broadcasted_iota(jnp.int32, (rows, HDIM), 0)
        local = []
        for b in range(PAIR):
            is_global = functools.reduce(
                jnp.logical_or, [pair * PAIR + b == block for block in glob_ids]
            )
            local.append(jnp.where(is_global, 0.0, 1.0))
        inv = jnp.where(row < BLK, local[0], local[1]) / total
        probs_ref[pair] = e
        inv_ref[pair] = inv
        attn_ref[pair] = (out[:, :HDIM] * inv).astype(jnp.bfloat16)
        return total

    def dense_pass(exact):
        q = jnp.concatenate(
            [block_rows(in_ref, block, 0, rows) for block in glob_ids], axis=0
        )
        if exact:
            top = jnp.full((globs * BLK, 1), NEG_FILL, jnp.float32)
            for c in range(devs):
                s = dot(q, in_ref[c, rows:2 * rows, :], NT)
                top = jnp.maximum(top, jnp.max(s, axis=1, keepdims=True))
        else:
            top = 0.0
        out = jnp.zeros((globs * BLK, 2 * HDIM), jnp.float32)
        ones = jnp.ones((2 * rows, HDIM), jnp.bfloat16)
        for c in range(devs // 2):
            keys = in_ref[2 * c:2 * c + 2, rows:2 * rows, :].reshape(2 * rows, HDIM)
            values = in_ref[2 * c:2 * c + 2, 2 * rows:3 * rows, :].reshape(2 * rows, HDIM)
            e = jnp.exp2((dot(q, keys, NT) - top) * EXP_FACTOR).astype(jnp.bfloat16)
            dense_ref[:, 2 * c * rows:2 * (c + 1) * rows] = e
            out = out + dot(e, jnp.concatenate([values, ones], axis=1))
        total = out[:, HDIM:]
        inv = 1.0 / total
        inv_dense_ref[...] = inv
        out = (out[:, :HDIM] * inv).astype(jnp.bfloat16)
        for t, block in enumerate(glob_ids):
            attn_ref[block // per, pl.ds(pl.multiple_of((block % per) * BLK, BLK), BLK), :] = (
                out[t * BLK:(t + 1) * BLK]
            )
        return total

    def single(pair, carry):
        pair_pass(pair, True)
        return carry

    totals = [pair_pass(pair, False) for pair in range(devs)] + [dense_pass(False)]
    low = jnp.min(functools.reduce(jnp.minimum, totals))
    high = jnp.max(functools.reduce(jnp.maximum, totals))
    in_range = (low > SUM_LOW) & (high < SUM_HIGH)

    @pl.when(jnp.logical_not(in_range))
    def _():
        lax.fori_loop(0, devs, single, 0)
        dense_pass(True)

    for i in range(devs):
        attn = attn_ref[i].astype(jnp.float32)
        grad = in_ref[i, 3 * rows:4 * rows, :].astype(jnp.float32) * gain_ref[...]
        square = jnp.sum((attn * attn).T, axis=0, keepdims=True)
        inner = jnp.sum((grad * attn).T, axis=0, keepdims=True)
        part_ref[i:i + 1, :] = jnp.concatenate([square, inner], axis=1)
    stats = part_ref[...].astype(stat_ref.dtype)
    for d in range(devs):
        stat_ref[d] = stats


def forward(slots, exchanged, bias, gain_row):
    devs, rows4, _ = exchanged.shape
    rows = rows4 // 4
    seq = devs * rows
    width = slots.shape[1] * BLK
    smem = pl.BlockSpec(memory_space=pltpu.SMEM)
    vmem = pl.BlockSpec(memory_space=pltpu.VMEM)
    return pl.pallas_call(
        forward_kernel,
        out_shape=[
            jax.ShapeDtypeStruct((devs, rows, width), jnp.bfloat16),
            jax.ShapeDtypeStruct((GLOB * BLK, seq), jnp.bfloat16),
            jax.ShapeDtypeStruct((devs, rows, HDIM), jnp.bfloat16),
            jax.ShapeDtypeStruct((devs, rows, HDIM), jnp.float32),
            jax.ShapeDtypeStruct((GLOB * BLK, HDIM), jnp.float32),
            jax.ShapeDtypeStruct((devs, devs, 2 * rows), jnp.bfloat16),
        ],
        in_specs=[smem, vmem, vmem, vmem],
        out_specs=[vmem] * 6,
        scratch_shapes=[pltpu.VMEM((devs, 2 * rows), jnp.float32)],
        compiler_params=pltpu.CompilerParams(vmem_limit_bytes=VMEM_LIMIT),
        name="forward",
    )(slots, exchanged, bias, gain_row)


def backward_kernel(
    slots_ref, in_ref, probs_ref, dense_ref, attn_ref, inv_ref, inv_dense_ref, stat_ref,
    gain_ref,
    out_ref, gain_out_ref,
    grad_ref, acc_ref, stage_ref, sems,
):
    devs, rows4, _ = in_ref.shape
    rows = rows4 // 4
    seq = devs * rows
    count = slots_ref.shape[1]
    globs = GLOB

    stats = stat_ref[0].astype(jnp.float32)
    for d in range(1, devs):
        stats = stats + stat_ref[d].astype(jnp.float32)
    stats = stats * (1.0 / (devs * HDIM))
    inv_rms = lax.rsqrt(stats[:, :rows] + EPSILON)
    shrink = inv_rms * inv_rms * stats[:, rows:]
    gain = jnp.zeros((8, HDIM), jnp.float32)
    for i in range(devs):
        factor = jnp.broadcast_to(inv_rms[i:i + 1], (HDIM, rows)).T
        minus = jnp.broadcast_to(shrink[i:i + 1], (HDIM, rows)).T
        attn = attn_ref[i].astype(jnp.float32)
        grad = in_ref[i, 3 * rows:4 * rows, :].astype(jnp.float32)
        grad_ref[i] = factor * (gain_ref[...] * grad - attn * minus)
        gain = gain + jnp.sum((grad * attn * factor).reshape(rows // 8, 8, HDIM), axis=0)
    gain_out_ref[...] = jnp.sum(gain, axis=0, keepdims=True)

    def block_of(ref, block, slot):
        return block_rows(ref, block, slot, rows)

    def side(low, q):
        zero = jnp.zeros_like(low)
        return jnp.concatenate(
            [jnp.concatenate([low, zero], axis=1), jnp.concatenate([zero, q], axis=1)], axis=0
        )

    def row_dot(low, attn):
        return jnp.sum(low.astype(jnp.float32) * attn.astype(jnp.float32), axis=1, keepdims=True)

    blocks = [slots_ref[0, GLOB_AT + t] for t in range(globs)]
    q = jnp.concatenate([block_of(in_ref, b, 0) for b in blocks], axis=0)
    low = jnp.concatenate([block_of(grad_ref, b, 0) for b in blocks], axis=0) * inv_dense_ref[...]
    low = low.astype(jnp.bfloat16)
    attn = jnp.concatenate([block_of(attn_ref, b, 0) for b in blocks], axis=0)
    both = side(low, q)
    dots = row_dot(low, attn)
    step = 512
    dq_dense = jnp.zeros((globs * BLK, HDIM), jnp.float32)
    for c in range(seq // step):
        values = in_ref[c * 4:(c + 1) * 4, 2 * rows:3 * rows, :].reshape(step, HDIM)
        keys = in_ref[c * 4:(c + 1) * 4, rows:2 * rows, :].reshape(step, HDIM)
        probs = dense_ref[:, c * step:(c + 1) * step]
        ds = (probs.astype(jnp.float32) * (dot(low, values, NT) - dots)).astype(jnp.bfloat16)
        dq_dense = dq_dense + dot(ds, keys)
        acc_ref[c * step:(c + 1) * step, :] = dot(jnp.concatenate([probs, ds], axis=0), both, TN)

    for pair in range(devs):
        ids = [slots_ref[pair, t] for t in range(count)]
        values = jnp.concatenate([block_of(in_ref, b, 2) for b in ids], axis=0)
        keys = jnp.concatenate([block_of(in_ref, b, 1) for b in ids], axis=0)
        q = in_ref[pair, 0:rows, :]
        low = (grad_ref[pair] * inv_ref[pair]).astype(jnp.bfloat16)
        probs = probs_ref[pair]
        dots = row_dot(low, attn_ref[pair])
        ds = (probs.astype(jnp.float32) * (dot(low, values, NT) - dots)).astype(jnp.bfloat16)
        stage_ref[pair, 0:rows, :] = (dot(ds, keys) * SCALE).astype(jnp.bfloat16)
        both = dot(jnp.concatenate([probs, ds], axis=0), side(low, q), TN)
        for t, block in enumerate(ids):
            acc_ref[pl.ds(pl.multiple_of(block * BLK, BLK), BLK), :] += (
                both[t * BLK:(t + 1) * BLK]
            )

    per = rows // BLK
    dq_dense = (dq_dense * SCALE).astype(jnp.bfloat16)
    for t, block in enumerate(blocks):
        stage_ref[block // per, pl.ds(pl.multiple_of((block % per) * BLK, BLK), BLK), :] = (
            dq_dense[t * BLK:(t + 1) * BLK]
        )
    copies = [
        pltpu.make_async_copy(stage_ref.at[:, 0:rows, :], out_ref.at[:, 0:rows, :], sems.at[0])
    ]
    copies[0].start()
    group = devs // PIECES
    for n in range(PIECES):
        for i in range(n * group, (n + 1) * group):
            span = slice(i * rows, (i + 1) * rows)
            stage_ref[i, rows:2 * rows, :] = (acc_ref[span, HDIM:] * SCALE).astype(jnp.bfloat16)
            stage_ref[i, 2 * rows:3 * rows, :] = acc_ref[span, :HDIM].astype(jnp.bfloat16)
        part = (slice(n * group, (n + 1) * group), slice(rows, 3 * rows))
        copies.append(
            pltpu.make_async_copy(stage_ref.at[*part], out_ref.at[*part], sems.at[n + 1])
        )
        copies[-1].start()
    for copy in copies:
        copy.wait()


def backward(slots, exchanged, forwarded, stats, gain_row):
    devs, rows4, _ = exchanged.shape
    rows = rows4 // 4
    seq = devs * rows
    smem = pl.BlockSpec(memory_space=pltpu.SMEM)
    vmem = pl.BlockSpec(memory_space=pltpu.VMEM)
    return pl.pallas_call(
        backward_kernel,
        out_shape=[
            pltpu.HBM((devs, 3 * rows, HDIM), jnp.bfloat16),
            jax.ShapeDtypeStruct((1, HDIM), jnp.float32),
        ],
        in_specs=[smem] + [vmem] * 8,
        out_specs=[pl.BlockSpec(memory_space=pltpu.HBM), vmem],
        scratch_shapes=[
            pltpu.VMEM((devs, rows, HDIM), jnp.float32),
            pltpu.VMEM((seq, 2 * HDIM), jnp.float32),
            pltpu.VMEM((devs, 3 * rows, HDIM), jnp.bfloat16),
            pltpu.SemaphoreType.DMA((PIECES + 1,)),
        ],
        compiler_params=pltpu.CompilerParams(vmem_limit_bytes=VMEM_LIMIT),
        name="backward",
    )(slots, exchanged, *forwarded, stats, gain_row)


def pair_slots(head_width, filing_globals, head_random, count):
    pairs = count // PAIR
    first = jnp.arange(pairs, dtype=jnp.int32)[:, None] * PAIR
    near = first + jnp.arange(-WMAX, PAIR + WMAX, dtype=jnp.int32)[None, :]
    globs = jnp.broadcast_to(filing_globals[None, :], (pairs, filing_globals.shape[0]))
    rand = head_random.reshape(pairs, -1)
    ids = jnp.concatenate([near, globs, rand], axis=1)
    total = ids.shape[1]
    inside = (ids >= 0) & (ids < count)
    earlier = jnp.arange(total)[:, None] > jnp.arange(total)[None, :]
    again = jnp.any((ids[:, :, None] == ids[:, None, :]) & earlier[None], axis=2)
    live = inside & jnp.logical_not(again)
    queries = first + jnp.arange(PAIR, dtype=jnp.int32)[None, :]
    per_query = head_random.reshape(pairs, PAIR, 1, -1)
    keys = ids[:, None, :]
    allowed = (
        (jnp.abs(keys - queries[:, :, None]) <= head_width)
        | jnp.any(keys[..., None] == filing_globals, axis=-1)
        | jnp.any(keys[..., None] == per_query, axis=-1)
    )
    bias = jnp.where(allowed & live[:, None, :], 0.0, NEG_FILL).astype(jnp.float32)
    bias = jnp.repeat(bias, BLK, axis=2)
    return jnp.clip(ids, 0, count - 1), bias


def body(
    query_rows, key_rows, value_rows, out_grad, norm_gains, window, global_blocks, random_blocks
):
    seq_count = lax.axis_size("seq")
    own_count = lax.axis_size("own")
    rows = query_rows.shape[1]
    seq = rows * seq_count
    gain_scale = (own_count * seq) ** (-0.5)
    exchange = functools.partial(
        lax.all_to_all, axis_name="seq", split_axis=0, concat_axis=0, tiled=True
    )
    exchanged = exchange(pack(query_rows, key_rows, value_rows, out_grad))
    gains = lax.all_gather(norm_gains, "own")
    gain_row = lax.dynamic_slice_in_dim(gains, lax.axis_index("seq"), 1, axis=0)
    slots, bias = pair_slots(window[0], global_blocks[0], random_blocks[0], seq // BLK)
    *forwarded, stats = forward(slots, exchanged, bias, gain_row)
    stats = exchange(stats)
    grads, gain_part = backward(slots, exchanged, forwarded, stats, gain_row)
    gain_terms = lax.all_gather(gain_part.reshape(-1), "own")
    gain_grad = jnp.sum(gain_terms, axis=0) * gain_scale
    out_query, out_key, out_value = unpack(exchange(grads))
    return (out_query, out_key, out_value, gain_grad)


def solution(mesh):
    rows = P("own", "seq", None)
    placed = (rows, rows, rows, rows, P("own"), P("seq"), P("own", None), P("seq", None, None))
    return jax.shard_map(
        body,
        mesh=mesh,
        in_specs=placed,
        out_specs=(rows, rows, rows, P("seq")),
        check_vma=False,
    )
```

```python
import functools
import math

import jax
import jax.numpy as jnp
from jax import lax
from jax.experimental import pallas as pl
from jax.experimental.pallas import tpu as pltpu
from jax.sharding import PartitionSpec as P

HDIM = 128
BLK = 64
WMAX = 2
PAIR = 2
GLOB = 2
GLOB_AT = PAIR + 2 * WMAX
PARTS = 2
PIECES = 2
NEG_FILL = -1e30
EPSILON = 1e-05
SCALE = 1.0 / math.sqrt(HDIM)
EXP_FACTOR = math.log2(math.e) * SCALE
VMEM_LIMIT = 40 * 1024 * 1024
SUM_LOW = 2.0 ** -80
SUM_HIGH = 2.0 ** 80
COPY_VMEM_LIMIT = 16 * 1024 * 1024

NT = (((1,), (1,)), ((), ()))
TN = (((0,), (0,)), ((), ()))


def dot(a, b, dims=None):
    if dims is None:
        return jnp.dot(a, b, preferred_element_type=jnp.float32)
    return lax.dot_general(a, b, dims, preferred_element_type=jnp.float32)


def pack_kernel(q_ref, k_ref, v_ref, g_ref, out_ref, raw_ref, stage_ref, in_sems, out_sems):
    heads = out_ref.shape[0]
    rows = q_ref.shape[1]
    part = rows // PARTS
    pieces = [(slot, c) for slot in range(4) for c in range(PARTS)]
    refs = (q_ref, k_ref, v_ref, g_ref)
    loads = [
        pltpu.make_async_copy(
            refs[slot].at[0, c * part:(c + 1) * part, :],
            raw_ref.at[slot, c * part:(c + 1) * part, :],
            in_sems.at[slot, c],
        )
        for slot, c in pieces
    ]
    for copy in loads:
        copy.start()
    stores = []
    for (slot, c), copy in zip(pieces, loads):
        copy.wait()
        span = slice(slot * rows + c * part, slot * rows + (c + 1) * part)
        for h in range(heads):
            stage_ref[h, span, :] = (
                raw_ref[slot, c * part:(c + 1) * part, h * HDIM:(h + 1) * HDIM]
            )
        stores.append(
            pltpu.make_async_copy(
                stage_ref.at[:, span, :], out_ref.at[:, span, :], out_sems.at[slot, c]
            )
        )
        stores[-1].start()
    for copy in stores:
        copy.wait()


def pack(query_rows, key_rows, value_rows, out_grad):
    _, rows, cols = query_rows.shape
    heads = cols // HDIM
    dtype = query_rows.dtype
    return pl.pallas_call(
        pack_kernel,
        out_shape=pltpu.HBM((heads, 4 * rows, HDIM), dtype),
        in_specs=[pl.BlockSpec(memory_space=pltpu.HBM)] * 4,
        out_specs=pl.BlockSpec(memory_space=pltpu.HBM),
        scratch_shapes=[
            pltpu.VMEM((4, rows, cols), dtype),
            pltpu.VMEM((heads, 4 * rows, HDIM), dtype),
            pltpu.SemaphoreType.DMA((4, PARTS)),
            pltpu.SemaphoreType.DMA((4, PARTS)),
        ],
        name="pack",
    )(query_rows, key_rows, value_rows, out_grad)


def unpack_kernel(in_ref, q_ref, k_ref, v_ref, stage_ref, sems):
    heads = in_ref.shape[0]
    rows = q_ref.shape[1]
    part = rows // PARTS
    copies = []
    for slot, ref in enumerate((q_ref, k_ref, v_ref)):
        for c in range(PARTS):
            span = slice(c * part, (c + 1) * part)
            for h in range(heads):
                stage_ref[slot, span, h * HDIM:(h + 1) * HDIM] = (
                    in_ref[h, slot * rows + c * part:slot * rows + (c + 1) * part, :]
                )
            copies.append(
                pltpu.make_async_copy(
                    stage_ref.at[slot, span, :], ref.at[0, span, :], sems.at[slot, c]
                )
            )
            copies[-1].start()
    for copy in copies:
        copy.wait()


def unpack(exchanged):
    heads, rows3, _ = exchanged.shape
    rows = rows3 // 3
    shape = jax.ShapeDtypeStruct((1, rows, heads * HDIM), exchanged.dtype)
    return pl.pallas_call(
        unpack_kernel,
        out_shape=[shape] * 3,
        in_specs=[pl.BlockSpec(memory_space=pltpu.VMEM)],
        out_specs=[pl.BlockSpec(memory_space=pltpu.HBM)] * 3,
        scratch_shapes=[
            pltpu.VMEM((3, rows, heads * HDIM), exchanged.dtype),
            pltpu.SemaphoreType.DMA((3, PARTS)),
        ],
        compiler_params=pltpu.CompilerParams(vmem_limit_bytes=COPY_VMEM_LIMIT),
        name="unpack",
    )(exchanged)


def block_rows(ref, block, slot, rows):
    per = rows // BLK
    offset = pl.multiple_of(slot * rows + (block % per) * BLK, BLK)
    return ref[block // per, pl.ds(offset, BLK), :]


def all_rows(ref, slot, rows):
    return ref[:, slot * rows:(slot + 1) * rows, :].reshape(ref.shape[0] * rows, HDIM)


def forward_kernel(
    slots_ref, in_ref, bias_ref, gain_ref,
    probs_ref, dense_ref, attn_ref, inv_ref, inv_dense_ref, stat_ref,
    part_ref,
):
    devs, rows4, _ = in_ref.shape
    rows = rows4 // 4
    count = slots_ref.shape[1]
    globs = GLOB
    glob_ids = [slots_ref[0, GLOB_AT + t] for t in range(globs)]
    per = rows // BLK

    def gather(pair, slot):
        return jnp.concatenate(
            [block_rows(in_ref, slots_ref[pair, t], slot, rows) for t in range(count)], axis=0
        )

    def pair_pass(pair, exact):
        s = dot(in_ref[pair, 0:rows, :], gather(pair, 1), NT)
        bias = bias_ref[pair]
        if exact:
            s = jnp.concatenate(
                [s[b * BLK:(b + 1) * BLK] + bias[b:b + 1] for b in range(PAIR)], axis=0
            )
            e = jnp.exp2((s - jnp.max(s, axis=1, keepdims=True)) * EXP_FACTOR)
        else:
            e = jnp.concatenate(
                [
                    jnp.exp2(s[b * BLK:(b + 1) * BLK] * EXP_FACTOR + bias[b:b + 1])
                    for b in range(PAIR)
                ],
                axis=0,
            )
        e = e.astype(jnp.bfloat16)
        values = jnp.concatenate(
            [gather(pair, 2), jnp.ones((count * BLK, HDIM), jnp.bfloat16)], axis=1
        )
        out = dot(e, values)
        total = out[:, HDIM:]
        row = lax.broadcasted_iota(jnp.int32, (rows, HDIM), 0)
        local = []
        for b in range(PAIR):
            is_global = functools.reduce(
                jnp.logical_or, [pair * PAIR + b == block for block in glob_ids]
            )
            local.append(jnp.where(is_global, 0.0, 1.0))
        inv = jnp.where(row < BLK, local[0], local[1]) / total
        probs_ref[pair] = e
        inv_ref[pair] = inv
        attn_ref[pair] = (out[:, :HDIM] * inv).astype(jnp.bfloat16)
        return total

    def dense_pass(exact):
        q = jnp.concatenate(
            [block_rows(in_ref, block, 0, rows) for block in glob_ids], axis=0
        )
        if exact:
            top = jnp.full((globs * BLK, 1), NEG_FILL, jnp.float32)
            for c in range(devs):
                s = dot(q, in_ref[c, rows:2 * rows, :], NT)
                top = jnp.maximum(top, jnp.max(s, axis=1, keepdims=True))
        else:
            top = 0.0
        out = jnp.zeros((globs * BLK, 2 * HDIM), jnp.float32)
        ones = jnp.ones((2 * rows, HDIM), jnp.bfloat16)
        for c in range(devs // 2):
            keys = in_ref[2 * c:2 * c + 2, rows:2 * rows, :].reshape(2 * rows, HDIM)
            values = in_ref[2 * c:2 * c + 2, 2 * rows:3 * rows, :].reshape(2 * rows, HDIM)
            e = jnp.exp2((dot(q, keys, NT) - top) * EXP_FACTOR).astype(jnp.bfloat16)
            dense_ref[:, 2 * c * rows:2 * (c + 1) * rows] = e
            out = out + dot(e, jnp.concatenate([values, ones], axis=1))
        total = out[:, HDIM:]
        inv = 1.0 / total
        inv_dense_ref[...] = inv
        out = (out[:, :HDIM] * inv).astype(jnp.bfloat16)
        for t, block in enumerate(glob_ids):
            attn_ref[block // per, pl.ds(pl.multiple_of((block % per) * BLK, BLK), BLK), :] = (
                out[t * BLK:(t + 1) * BLK]
            )
        return total

    def single(pair, carry):
        pair_pass(pair, True)
        return carry

    totals = [pair_pass(pair, False) for pair in range(devs)] + [dense_pass(False)]
    low = jnp.min(functools.reduce(jnp.minimum, totals))
    high = jnp.max(functools.reduce(jnp.maximum, totals))
    in_range = (low > SUM_LOW) & (high < SUM_HIGH)

    @pl.when(jnp.logical_not(in_range))
    def _():
        lax.fori_loop(0, devs, single, 0)
        dense_pass(True)

    for i in range(devs):
        attn = attn_ref[i].astype(jnp.float32)
        grad = in_ref[i, 3 * rows:4 * rows, :].astype(jnp.float32) * gain_ref[...]
        square = jnp.sum((attn * attn).T, axis=0, keepdims=True)
        inner = jnp.sum((grad * attn).T, axis=0, keepdims=True)
        part_ref[i:i + 1, :] = jnp.concatenate([square, inner], axis=1)
    stats = part_ref[...].astype(stat_ref.dtype)
    for d in range(devs):
        stat_ref[d] = stats


def forward(slots, exchanged, bias, gain_row):
    devs, rows4, _ = exchanged.shape
    rows = rows4 // 4
    seq = devs * rows
    width = slots.shape[1] * BLK
    smem = pl.BlockSpec(memory_space=pltpu.SMEM)
    vmem = pl.BlockSpec(memory_space=pltpu.VMEM)
    return pl.pallas_call(
        forward_kernel,
        out_shape=[
            jax.ShapeDtypeStruct((devs, rows, width), jnp.bfloat16),
            jax.ShapeDtypeStruct((GLOB * BLK, seq), jnp.bfloat16),
            jax.ShapeDtypeStruct((devs, rows, HDIM), jnp.bfloat16),
            jax.ShapeDtypeStruct((devs, rows, HDIM), jnp.float32),
            jax.ShapeDtypeStruct((GLOB * BLK, HDIM), jnp.float32),
            jax.ShapeDtypeStruct((devs, devs, 2 * rows), jnp.bfloat16),
        ],
        in_specs=[smem, vmem, vmem, vmem],
        out_specs=[vmem] * 6,
        scratch_shapes=[pltpu.VMEM((devs, 2 * rows), jnp.float32)],
        compiler_params=pltpu.CompilerParams(vmem_limit_bytes=VMEM_LIMIT),
        name="forward",
    )(slots, exchanged, bias, gain_row)


def backward_kernel(
    slots_ref, in_ref, probs_ref, dense_ref, attn_ref, inv_ref, inv_dense_ref, stat_ref,
    gain_ref,
    out_ref, gain_out_ref,
    grad_ref, acc_ref, stage_ref, sems,
):
    devs, rows4, _ = in_ref.shape
    rows = rows4 // 4
    seq = devs * rows
    count = slots_ref.shape[1]
    globs = GLOB

    stats = stat_ref[0].astype(jnp.float32)
    for d in range(1, devs):
        stats = stats + stat_ref[d].astype(jnp.float32)
    stats = stats * (1.0 / (devs * HDIM))
    inv_rms = lax.rsqrt(stats[:, :rows] + EPSILON)
    shrink = inv_rms * inv_rms * stats[:, rows:]
    gain = jnp.zeros((8, HDIM), jnp.float32)
    for i in range(devs):
        factor = jnp.broadcast_to(inv_rms[i:i + 1], (HDIM, rows)).T
        minus = jnp.broadcast_to(shrink[i:i + 1], (HDIM, rows)).T
        attn = attn_ref[i].astype(jnp.float32)
        grad = in_ref[i, 3 * rows:4 * rows, :].astype(jnp.float32)
        grad_ref[i] = factor * (gain_ref[...] * grad - attn * minus)
        gain = gain + jnp.sum((grad * attn * factor).reshape(rows // 8, 8, HDIM), axis=0)
    gain_out_ref[...] = jnp.sum(gain, axis=0, keepdims=True)

    def block_of(ref, block, slot):
        return block_rows(ref, block, slot, rows)

    def side(low, q):
        zero = jnp.zeros_like(low)
        return jnp.concatenate(
            [jnp.concatenate([low, zero], axis=1), jnp.concatenate([zero, q], axis=1)], axis=0
        )

    def row_dot(low, attn):
        return jnp.sum(low.astype(jnp.float32) * attn.astype(jnp.float32), axis=1, keepdims=True)

    blocks = [slots_ref[0, GLOB_AT + t] for t in range(globs)]
    q = jnp.concatenate([block_of(in_ref, b, 0) for b in blocks], axis=0)
    low = jnp.concatenate([block_of(grad_ref, b, 0) for b in blocks], axis=0) * inv_dense_ref[...]
    low = low.astype(jnp.bfloat16)
    attn = jnp.concatenate([block_of(attn_ref, b, 0) for b in blocks], axis=0)
    both = side(low, q)
    dots = row_dot(low, attn)
    step = 1024
    dq_dense = jnp.zeros((globs * BLK, HDIM), jnp.float32)
    for c in range(seq // step):
        values = in_ref[c * 8:(c + 1) * 8, 2 * rows:3 * rows, :].reshape(step, HDIM)
        keys = in_ref[c * 8:(c + 1) * 8, rows:2 * rows, :].reshape(step, HDIM)
        probs = dense_ref[:, c * step:(c + 1) * step]
        ds = (probs.astype(jnp.float32) * (dot(low, values, NT) - dots)).astype(jnp.bfloat16)
        dq_dense = dq_dense + dot(ds, keys)
        acc_ref[c * step:(c + 1) * step, :] = dot(jnp.concatenate([probs, ds], axis=0), both, TN)

    for pair in range(devs):
        ids = [slots_ref[pair, t] for t in range(count)]
        values = jnp.concatenate([block_of(in_ref, b, 2) for b in ids], axis=0)
        keys = jnp.concatenate([block_of(in_ref, b, 1) for b in ids], axis=0)
        q = in_ref[pair, 0:rows, :]
        low = (grad_ref[pair] * inv_ref[pair]).astype(jnp.bfloat16)
        probs = probs_ref[pair]
        dots = row_dot(low, attn_ref[pair])
        ds = (probs.astype(jnp.float32) * (dot(low, values, NT) - dots)).astype(jnp.bfloat16)
        stage_ref[pair, 0:rows, :] = (dot(ds, keys) * SCALE).astype(jnp.bfloat16)
        both = dot(jnp.concatenate([probs, ds], axis=0), side(low, q), TN)
        for t, block in enumerate(ids):
            acc_ref[pl.ds(pl.multiple_of(block * BLK, BLK), BLK), :] += (
                both[t * BLK:(t + 1) * BLK]
            )

    per = rows // BLK
    dq_dense = (dq_dense * SCALE).astype(jnp.bfloat16)
    for t, block in enumerate(blocks):
        stage_ref[block // per, pl.ds(pl.multiple_of((block % per) * BLK, BLK), BLK), :] = (
            dq_dense[t * BLK:(t + 1) * BLK]
        )
    copies = [
        pltpu.make_async_copy(stage_ref.at[:, 0:rows, :], out_ref.at[:, 0:rows, :], sems.at[0])
    ]
    copies[0].start()
    group = devs // PIECES
    for n in range(PIECES):
        for i in range(n * group, (n + 1) * group):
            span = slice(i * rows, (i + 1) * rows)
            stage_ref[i, rows:2 * rows, :] = (acc_ref[span, HDIM:] * SCALE).astype(jnp.bfloat16)
            stage_ref[i, 2 * rows:3 * rows, :] = acc_ref[span, :HDIM].astype(jnp.bfloat16)
        part = (slice(n * group, (n + 1) * group), slice(rows, 3 * rows))
        copies.append(
            pltpu.make_async_copy(stage_ref.at[*part], out_ref.at[*part], sems.at[n + 1])
        )
        copies[-1].start()
    for copy in copies:
        copy.wait()


def backward(slots, exchanged, forwarded, stats, gain_row):
    devs, rows4, _ = exchanged.shape
    rows = rows4 // 4
    seq = devs * rows
    smem = pl.BlockSpec(memory_space=pltpu.SMEM)
    vmem = pl.BlockSpec(memory_space=pltpu.VMEM)
    return pl.pallas_call(
        backward_kernel,
        out_shape=[
            pltpu.HBM((devs, 3 * rows, HDIM), jnp.bfloat16),
            jax.ShapeDtypeStruct((1, HDIM), jnp.float32),
        ],
        in_specs=[smem] + [vmem] * 8,
        out_specs=[pl.BlockSpec(memory_space=pltpu.HBM), vmem],
        scratch_shapes=[
            pltpu.VMEM((devs, rows, HDIM), jnp.float32),
            pltpu.VMEM((seq, 2 * HDIM), jnp.float32),
            pltpu.VMEM((devs, 3 * rows, HDIM), jnp.bfloat16),
            pltpu.SemaphoreType.DMA((PIECES + 1,)),
        ],
        compiler_params=pltpu.CompilerParams(vmem_limit_bytes=VMEM_LIMIT),
        name="backward",
    )(slots, exchanged, *forwarded, stats, gain_row)


def pair_slots(head_width, filing_globals, head_random, count):
    pairs = count // PAIR
    first = jnp.arange(pairs, dtype=jnp.int32)[:, None] * PAIR
    near = first + jnp.arange(-WMAX, PAIR + WMAX, dtype=jnp.int32)[None, :]
    globs = jnp.broadcast_to(filing_globals[None, :], (pairs, filing_globals.shape[0]))
    rand = head_random.reshape(pairs, -1)
    ids = jnp.concatenate([near, globs, rand], axis=1)
    total = ids.shape[1]
    inside = (ids >= 0) & (ids < count)
    earlier = jnp.arange(total)[:, None] > jnp.arange(total)[None, :]
    again = jnp.any((ids[:, :, None] == ids[:, None, :]) & earlier[None], axis=2)
    live = inside & jnp.logical_not(again)
    queries = first + jnp.arange(PAIR, dtype=jnp.int32)[None, :]
    per_query = head_random.reshape(pairs, PAIR, 1, -1)
    keys = ids[:, None, :]
    allowed = (
        (jnp.abs(keys - queries[:, :, None]) <= head_width)
        | jnp.any(keys[..., None] == filing_globals, axis=-1)
        | jnp.any(keys[..., None] == per_query, axis=-1)
    )
    bias = jnp.where(allowed & live[:, None, :], 0.0, NEG_FILL).astype(jnp.float32)
    bias = jnp.repeat(bias, BLK, axis=2)
    return jnp.clip(ids, 0, count - 1), bias


def body(
    query_rows, key_rows, value_rows, out_grad, norm_gains, window, global_blocks, random_blocks
):
    seq_count = lax.axis_size("seq")
    own_count = lax.axis_size("own")
    rows = query_rows.shape[1]
    seq = rows * seq_count
    gain_scale = (own_count * seq) ** (-0.5)
    exchange = functools.partial(
        lax.all_to_all, axis_name="seq", split_axis=0, concat_axis=0, tiled=True
    )
    exchanged = exchange(pack(query_rows, key_rows, value_rows, out_grad))
    gains = lax.all_gather(norm_gains, "own")
    gain_row = lax.dynamic_slice_in_dim(gains, lax.axis_index("seq"), 1, axis=0)
    slots, bias = pair_slots(window[0], global_blocks[0], random_blocks[0], seq // BLK)
    *forwarded, stats = forward(slots, exchanged, bias, gain_row)
    stats = exchange(stats)
    grads, gain_part = backward(slots, exchanged, forwarded, stats, gain_row)
    gain_terms = lax.all_gather(gain_part.reshape(-1), "own")
    gain_grad = jnp.sum(gain_terms, axis=0) * gain_scale
    out_query, out_key, out_value = unpack(exchange(grads))
    return (out_query, out_key, out_value, gain_grad)


def solution(mesh):
    rows = P("own", "seq", None)
    placed = (rows, rows, rows, rows, P("own"), P("seq"), P("own", None), P("seq", None, None))
    return jax.shard_map(
        body,
        mesh=mesh,
        in_specs=placed,
        out_specs=(rows, rows, rows, P("seq")),
        check_vma=False,
    )
```
